128 devices in a mesh: bx: 8 (over y_lo, z), by: 16 (over y_hi, x, core).
Axes of the slice: x: 4, y: 4 (y_hi: 2, y_lo: 2; y = y_hi * 2 + y_lo), z: 4, core: 2. Of those that a mesh axis runs over, the one named last changes fastest.
Arguments:
- populations: float32 [19, 256, 512, 128], P(None, 'bx', 'by'), may hold values from 0.2 to 8, as said below
- fluid_mask: int32 [256, 512, 128], P('bx', 'by'), may hold values from 0 to 1, as said below
- rate_class: int32 [256, 512, 128], P('bx', 'by'), may hold values from 0 to 3
- class_rates: float32 [4], replicated, may hold values from 0.6 to 1.8
Outputs:
- final_populations: float32 [19, 256, 512, 128], P(None, 'bx', 'by')
- mean_flow: float32 [1], replicated
The draws below stay inside these ranges and needn't reach their ends.
Inputs may be any that keep to these rules, and one draw needn't show every extreme that they name: `fluid_mask`: at least one cell is fluid. `populations`: every population is positive.
All inputs are finite; a program needn't handle non-finite values.
Results may differ from the reference program's by a relative error of at most 0.00002.
Values sent between devices are 32-bit elements; how exact they have to be, the bound alone decides.
No kernel may reach another device: no remote copies, remote signals or barrier semaphores. Data moves between devices by JAX's collectives and lax.ppermute only.
A program may use at most 192 MiB of HBM per device.

```python
import jax
import jax.numpy as jnp

TILE = 32
ITERS = 2
NCLASS = 4
NX = 256
NY = 512
NZ = 128


VELOCITY = [(0, 0, 0), (1, 0, 0), (-1, 0, 0), (0, 1, 0), (0, -1, 0), (0, 0, 1), (0, 0, -1), (1, 1, 0), (-1, -1, 0), (1, -1, 0), (-1, 1, 0), (1, 0, 1), (-1, 0, -1), (1, 0, -1), (-1, 0, 1), (0, 1, 1), (0, -1, -1), (0, 1, -1), (0, -1, 1)]


WEIGHT_TABLE = [1.0 / 3.0] + [1.0 / 18.0] * 6 + [1.0 / 36.0] * 12


def draw_populations(key, part):
    key = jax.random.fold_in(key, 5)
    shape = (19, NX, NY, NZ)
    weights = jnp.array(WEIGHT_TABLE, jnp.float32)[:, None, None, None]
    along_z = jnp.array([float(move[2]) for move in VELOCITY], jnp.float32)[:, None, None, None]
    position = (jnp.arange(NX, dtype=jnp.float32) / NX)[None, :, None, None]
    noise = 0.1 * jnp.clip(jax.random.normal(key, shape, jnp.float32), -3.0, 3.0)
    drift = 0.08 + 0.0 * position
    along = along_z * drift
    base = 18.0 * weights * (1.0 + 3.0 * along + 4.5 * along * along - 1.5 * drift * drift)
    return base * (1.0 + noise)


def draw_fluid_mask(key, part):
    key = jax.random.fold_in(key, 11)
    cell_key, block_key = jax.random.split(key)
    row = jnp.arange(NX, dtype=jnp.int32)[:, None, None]
    cell_pct = 25 + 50 * row // NX
    cells = jax.random.randint(cell_key, (NX, NY, NZ), 0, 100) < cell_pct
    block_row = jnp.arange(NX // TILE, dtype=jnp.int32)[:, None, None]
    block_pct = 40 - 40 * block_row * TILE // NX
    blocks = jax.random.randint(block_key, (NX // TILE, NY // TILE, NZ // TILE), 0, 100) < block_pct
    rock = jnp.repeat(jnp.repeat(jnp.repeat(blocks, TILE, axis=0), TILE, axis=1), TILE, axis=2)
    ycol = jnp.arange(NY, dtype=jnp.int32)[None, :, None]
    zcol = jnp.arange(NZ, dtype=jnp.int32)[None, None, :]
    corner = (row == NX - 1) & (ycol == 0) & (zcol == 0)
    fluid = cells & jnp.logical_not(rock) | corner
    return fluid.astype(jnp.int32)


def with_ends(entries, rng, low, largest):
    index_at = [jax.random.randint(jax.random.fold_in(rng, axis), (), 0, length) for axis, length in enumerate(entries.shape)]
    main_axis = entries.shape.index(max(entries.shape))
    next_to = index_at[:main_axis] + [(index_at[main_axis] + 1) % entries.shape[main_axis]] + index_at[main_axis + 1:]
    return entries.at[tuple(index_at)].set(low).at[tuple(next_to)].set(largest)


def setup_inputs(seed: int = 0) -> dict:
    seeds = jax.random.split(jax.random.key(seed), 5)
    populations = draw_populations(jax.random.fold_in(seeds[4], 71), 0)
    fluid_mask = draw_fluid_mask(jax.random.fold_in(seeds[4], 71), 0)
    rate_class = with_ends(jax.random.randint(seeds[2], (NX, NY, NZ), 0, NCLASS), jax.random.fold_in(seeds[2], 1), 0, NCLASS - 1).astype(jnp.int32)
    class_rates = jnp.clip(jax.random.uniform(seeds[3], (NCLASS,), jnp.float32, 0.6, 1.8), 0.6, 1.8)
    return {"populations": populations, "fluid_mask": fluid_mask, "rate_class": rate_class, "class_rates": class_rates}


VELOCITY = [(0, 0, 0), (1, 0, 0), (-1, 0, 0), (0, 1, 0), (0, -1, 0), (0, 0, 1), (0, 0, -1),
            (1, 1, 0), (-1, -1, 0), (1, -1, 0), (-1, 1, 0), (1, 0, 1), (-1, 0, -1), (1, 0, -1), (-1, 0, 1),
            (0, 1, 1), (0, -1, -1), (0, 1, -1), (0, -1, 1)]
WEIGHT_TABLE = [1.0 / 3.0] + [1.0 / 18.0] * 6 + [1.0 / 36.0] * 12
OPPOSITE = [0, 2, 1, 4, 3, 6, 5, 8, 7, 10, 9, 12, 11, 14, 13, 16, 15, 18, 17]


def signed_total(comps, axis_pick):
    total = None
    for index in range(19):
        coef = VELOCITY[index][axis_pick]
        if coef == 0:
            continue
        term = comps[index] if coef > 0 else -comps[index]
        total = term if total is None else total + term
    return total


def rate_field(rate_class, class_rates):
    rate = jnp.zeros(rate_class.shape, class_rates.dtype)
    for level in range(class_rates.shape[0]):
        rate = rate + jnp.where(rate_class == level, class_rates[level], 0.0)
    return rate


def collide(populations, fluid, rate):
    comps = [populations[index] for index in range(19)]
    density = comps[0]
    for index in range(1, 19):
        density = density + comps[index]
    speed_x = signed_total(comps, 0) / density
    speed_y = signed_total(comps, 1) / density
    speed_z = signed_total(comps, 2) / density
    speeds = (speed_x, speed_y, speed_z)
    square = speed_x * speed_x + speed_y * speed_y + speed_z * speed_z
    result = []
    for index in range(19):
        along = None
        for axis_pick in range(3):
            coef = VELOCITY[index][axis_pick]
            if coef == 0:
                continue
            term = speeds[axis_pick] if coef > 0 else -speeds[axis_pick]
            along = term if along is None else along + term
        if along is None:
            equil = WEIGHT_TABLE[index] * density * (1.0 - 1.5 * square)
        else:
            equil = WEIGHT_TABLE[index] * density * (1.0 + 3.0 * along + 4.5 * along * along - 1.5 * square)
        result.append(jnp.where(fluid, comps[index] + rate * (equil - comps[index]), comps[index]))
    return jnp.stack(result)


def reference(populations, fluid_mask, rate_class, class_rates):
    fluid = fluid_mask == 1
    rate = rate_field(rate_class, class_rates)
    state = populations
    for step in range(ITERS):
        post = collide(state, fluid, rate)
        result = []
        for index in range(19):
            move = VELOCITY[index]
            if index == 0:
                result.append(post[0])
                continue
            source = jnp.roll(post[index], move, axis=(0, 1, 2))
            source_fluid = jnp.roll(fluid, move, axis=(0, 1, 2))
            inner = jnp.where(source_fluid, source, post[OPPOSITE[index]])
            result.append(jnp.where(fluid, inner, post[index]))
        state = jnp.stack(result)
    momentum = signed_total([state[index] for index in range(19)], 2)
    total_flux = jnp.sum(jnp.where(fluid, momentum, 0.0))
    total_count = jnp.sum(fluid.astype(state.dtype))
    return state, (total_flux / total_count).reshape(1)
```

```python
import jax
import jax.numpy as jnp
from jax import lax
from jax.experimental import pallas as pl
from jax.experimental.pallas import tpu as pltpu
from jax.sharding import PartitionSpec as P

VELOCITY = [
    (0, 0, 0),
    (1, 0, 0),
    (-1, 0, 0),
    (0, 1, 0),
    (0, -1, 0),
    (0, 0, 1),
    (0, 0, -1),
    (1, 1, 0),
    (-1, -1, 0),
    (1, -1, 0),
    (-1, 1, 0),
    (1, 0, 1),
    (-1, 0, -1),
    (1, 0, -1),
    (-1, 0, 1),
    (0, 1, 1),
    (0, -1, -1),
    (0, 1, -1),
    (0, -1, 1),
]
OPPOSITE = [0, 2, 1, 4, 3, 6, 5, 8, 7, 10, 9, 12, 11, 14, 13, 16, 15, 18, 17]
UP_X = [q for q in range(19) if VELOCITY[q][0] == 1]
DOWN_X = [OPPOSITE[q] for q in UP_X]
UP_Y = [q for q in range(19) if VELOCITY[q][1] == 1]
DOWN_Y = [OPPOSITE[q] for q in UP_Y]
CORNERS = [(7, 1, 1), (8, -1, -1), (9, 1, -1), (10, -1, 1)]

OFF = 8
F32 = jnp.float32
MIB = 1024 * 1024


def collide(f, rate):
    plus = {}
    diff = {}
    for q in range(1, 19, 2):
        plus[q] = f[q] + f[q + 1]
        diff[q] = f[q] - f[q + 1]
    rho = ((f[0] + plus[1]) + (plus[3] + plus[5])) + (
        ((plus[7] + plus[9]) + (plus[11] + plus[13])) + (plus[15] + plus[17])
    )
    mx = (diff[1] + diff[7]) + (diff[9] + diff[11]) + diff[13]
    my = (diff[3] + diff[7]) + (diff[15] - diff[9]) + diff[17]
    mz = (diff[5] + diff[11]) + (diff[15] - diff[13]) - diff[17]
    inv = 4.5 / rho
    ux = inv * mx
    uy = inv * my
    uz = inv * mz
    tx = ux * mx
    ty = uy * my
    tz = uz * mz
    base = rho - ((tx + ty) + tz) * (1.0 / 3.0)
    keep = 1.0 - rate
    r36 = rate * (1.0 / 36.0)
    r18 = rate * (1.0 / 18.0)
    r12 = rate * (1.0 / 12.0)
    gx = r12 * mx
    gy = r12 * my
    gz = r12 * mz
    ux2 = ux + ux
    uy2 = uy + uy
    cross = {7: ux2 * my, 11: ux2 * mz, 15: uy2 * mz}
    pair_base = {7: base + (tx + ty), 11: base + (tx + tz), 15: base + (ty + tz)}
    lean = {7: (gx, gy), 11: (gx, gz), 15: (gy, gz)}
    out = [None] * 19
    out[0] = keep * f[0] + (rate * (1.0 / 3.0)) * base
    for q, t, g in ((1, tx, gx), (3, ty, gy), (5, tz, gz)):
        even = r18 * (base + t)
        odd = g + g
        out[q] = keep * f[q] + (even + odd)
        out[q + 1] = keep * f[q + 1] + (even - odd)
    for q in (7, 11, 15):
        one, two = lean[q]
        even = r36 * (pair_base[q] + cross[q])
        odd = one + two
        out[q] = keep * f[q] + (even + odd)
        out[q + 1] = keep * f[q + 1] + (even - odd)
        even = r36 * (pair_base[q] - cross[q])
        odd = one - two
        out[q + 2] = keep * f[q + 2] + (even + odd)
        out[q + 3] = keep * f[q + 3] + (even - odd)
    return out, mz


def turn(value, step):
    if step == 0:
        return value
    return pltpu.roll(value, step % value.shape[-1], axis=value.ndim - 1)


def cell_rate(cls, fluid, rates):
    rate = jnp.where(cls == 0, rates[0], rates[1])
    rate = jnp.where(cls == 2, rates[2], rate)
    rate = jnp.where(cls == 3, rates[3], rate)
    return jnp.where(fluid, rate, 0.0)


def pull(local, load, is_open):
    out = [local[0]]
    links = [None]
    for q in range(1, 19):
        move = VELOCITY[q]
        source = local[q] if move[0] == 0 and move[1] == 0 else load(q, move[0], move[1])
        links.append(is_open(q))
        out.append(jnp.where(links[q], turn(source, move[2]), local[OPPOSITE[q]]))
    return out, links


def open_by_flag(load_flag, fluid):
    limit = jnp.where(fluid > 0.5, 0.5, 2.0)

    def is_open(q):
        move = VELOCITY[q]
        return load_flag(move[2], move[0], move[1]) > limit

    return is_open


def link_flux(post, links, mz, fluid):
    total = None
    for q in range(19):
        step = VELOCITY[q][2]
        if step == 0:
            continue
        term = jnp.where(links[OPPOSITE[q]], post[q], 0.0)
        if total is None:
            total = term if step > 0 else -term
        else:
            total = total + term if step > 0 else total - term
    return (total + total) - jnp.where(fluid > 0.5, mz, 0.0)


def shifted(read, g, groups, cy, low, high):
    if cy == 1 and g == 0:
        value = pltpu.roll(read(tile(g)), 1, axis=0)
        return jnp.where(lax.broadcasted_iota(jnp.int32, value.shape, 0) == 0, low(), value)
    if cy == -1 and g == groups - 1:
        value = pltpu.roll(read(tile(g)), 7, axis=0)
        return jnp.where(lax.broadcasted_iota(jnp.int32, value.shape, 0) == 7, high(), value)
    return read(pl.ds(g * 8 - cy, 8))


def side_row(halo_ref, x, q):
    k = UP_Y.index(q) if q in UP_Y else 5 + DOWN_Y.index(q)
    return halo_ref[k, pl.ds(x, 1), :]


def tile(g):
    return pl.ds(g * 8, 8)


def parity(axis):
    return lax.rem(lax.axis_index(axis), 2)


def device_at(dx, dy):
    size_x = lax.axis_size("bx")
    size_y = lax.axis_size("by")
    at_x = lax.rem(lax.axis_index("bx") + (dx + size_x), size_x)
    at_y = lax.rem(lax.axis_index("by") + (dy + size_y), size_y)
    return at_x * size_y + at_y


def first_faces(
    f_hbm, mask_hbm, cls_hbm, rates_hbm, far_ref, near_ref,
    f_buf, mask_buf, cls_buf, rates_ref, sems, rates_sem,
):
    odd = parity("by")
    width = f_hbm.shape[1]
    length = f_hbm.shape[2]
    get_rates = pltpu.make_async_copy(rates_hbm, rates_ref, rates_sem)
    get_rates.start()
    copies = []
    for side in range(2):
        src = pl.ds(side * (length - 1), 1)
        group = [
            pltpu.make_async_copy(f_hbm.at[:, :, src, :], f_buf.at[side], sems.at[side, 0]),
            pltpu.make_async_copy(mask_hbm.at[:, src, :], mask_buf.at[side], sems.at[side, 1]),
            pltpu.make_async_copy(cls_hbm.at[:, src, :], cls_buf.at[side], sems.at[side, 2]),
        ]
        for copy in group:
            copy.start()
        copies.append(group)
    get_rates.wait()
    rates = [rates_ref[k] for k in range(4)]
    leaving = []
    for side in range(2):
        for copy in copies[side]:
            copy.wait()
        f_rows = f_buf.at[side].reshape(19, width, 128)
        mask_rows = mask_buf.at[side].reshape(width, 128)
        cls_rows = cls_buf.at[side].reshape(width, 128)
        for g in range(width // 8):
            fluid = mask_rows[tile(g), :] == 1
            rate = cell_rate(cls_rows[tile(g), :], fluid, rates)
            post, _ = collide([f_rows[q, tile(g), :] for q in range(19)], rate)
            values = [post[q] for q in (UP_Y if side else DOWN_Y)]
            leaving.append(values + [jnp.where(fluid, 1.0, 0.0)])
    for g in range(width // 8):
        for k in range(6):
            low = leaving[g][k]
            high = leaving[width // 8 + g][k]
            far_ref[k, tile(g), :] = jnp.where(odd == 0, low, high)
            near_ref[k, tile(g), :] = jnp.where(odd == 0, high, low)


def first_step(
    f_hbm, mask_hbm, cls_hbm, rates_hbm, order_ref,
    post_ref, flag_ref, flag_hbm, rate_ref, edge_ref, edge_flag, edge_rate, face_ref,
    f_buf, mask_ref, cls_ref, rates_ref, sems, small_sems, flag_sems,
):
    del order_ref
    width, length = mask_ref.shape[:2]
    groups = length // 8
    chunk = width // sems.shape[0]
    ahead = 4
    small = [
        pltpu.make_async_copy(rates_hbm, rates_ref, small_sems.at[0]),
        pltpu.make_async_copy(mask_hbm, mask_ref, small_sems.at[1]),
        pltpu.make_async_copy(cls_hbm, cls_ref, small_sems.at[2]),
    ]

    def fetch(c):
        planes = pl.ds(c * chunk, chunk)
        return pltpu.make_async_copy(f_hbm.at[:, planes], f_buf.at[:, planes], sems.at[c])

    def keep(c):
        planes = pl.ds(c * chunk, chunk)
        return pltpu.make_async_copy(flag_ref.at[:, planes], flag_hbm.at[:, planes], flag_sems.at[c])

    for copy in small:
        copy.start()
    for c in range(ahead):
        fetch(c).start()
    for copy in small:
        copy.wait()
    rates = [rates_ref[k] for k in range(4)]

    def part(c, carry):
        fetch(c).wait()

        @pl.when(c + ahead < width // chunk)
        def _():
            fetch(c + ahead).start()

        def plane(x, carry):
            for g in range(groups):
                fluid = mask_ref[x, tile(g), :] == 1
                rate = cell_rate(cls_ref[x, tile(g), :], fluid, rates)
                post, _ = collide([f_buf[q, x, tile(g), :] for q in range(19)], rate)
                for q in range(19):
                    post_ref[q, x, tile(g), :] = post[q]
                rate_ref[x, tile(g), :] = rate
                flag = jnp.where(fluid, 1.0, 0.0)
                for step in (-1, 0, 1):
                    flag_ref[step + 1, x, tile(g), :] = turn(flag, step)
            return carry

        lax.fori_loop(c * chunk, (c + 1) * chunk, plane, 0)
        keep(c).start()
        return carry

    lax.fori_loop(0, width // chunk, part, 0)
    for e, x in enumerate((0, 1, width - 2, width - 1)):
        for g in range(groups):
            for q in range(19):
                edge_ref[q, e, tile(g), :] = post_ref[q, x, tile(g), :]
            for s in range(3):
                edge_flag[s, e, tile(g), :] = flag_ref[s, x, tile(g), :]
    for s, x in enumerate((0, width - 1)):
        leaving = UP_X if s else DOWN_X
        for g in range(groups):
            edge_rate[s, tile(g), :] = rate_ref[x, tile(g), :]
            for k in range(5):
                face_ref[s * 6 + k, tile(g), :] = post_ref[leaving[k], x, tile(g), :]
            face_ref[s * 6 + 5, tile(g), :] = flag_ref[1, x, tile(g), :]

    def finish(c, carry):
        keep(c).wait()
        return carry

    lax.fori_loop(0, width // chunk, finish, 0)


def join_sides(
    face_ref, far_ref, near_ref,
    far_out, near_out, halo_ref, flag_ref, halo_edge, flag_edge, flag_last,
):
    odd_x = parity("bx")
    odd_y = parity("by")
    width = far_ref.shape[1]
    length = face_ref.shape[1]
    for g in range(width // 8):
        for k in range(6):
            far = far_ref[k, tile(g), :]
            near = near_ref[k, tile(g), :]
            low = jnp.where(odd_y == 0, far, near)
            high = jnp.where(odd_y == 0, near, far)
            if k < 5:
                for out_ref in (halo_ref, halo_edge):
                    out_ref[k, tile(g), :] = low
                    out_ref[5 + k, tile(g), :] = high
                continue
            for step in (-1, 0, 1):
                for side, value in enumerate((low, high)):
                    turned = turn(value, step)
                    for out_ref in (flag_ref, flag_edge, flag_last):
                        out_ref[(step + 1) * 2 + side, tile(g), :] = turned
    def put(k, at, low, high):
        far_out[k, at, :] = jnp.where(odd_x == 0, low, high)
        near_out[k, at, :] = jnp.where(odd_x == 0, high, low)

    for k in range(6):
        for g in range(length // 8):
            put(k, pl.ds(1 + g * 8, 8), face_ref[k, tile(g), :], face_ref[6 + k, tile(g), :])
        if k == 5:
            for side in range(2):
                ends = [halo_row(flag_ref, 2 + side, x) for x in (0, width - 1)]
                put(k, pl.ds(side * (length + 1), 1), *ends)
            continue
        q = DOWN_X[k]
        if q in UP_Y:
            bottom, top = side_row(halo_ref, 0, q), side_row(halo_ref, width - 1, OPPOSITE[q])
        elif q in DOWN_Y:
            bottom, top = side_row(halo_ref, width - 1, OPPOSITE[q]), side_row(halo_ref, 0, q)
        else:
            continue
        put(k, pl.ds(0, 1), bottom, bottom)
        put(k, pl.ds(length + 1, 1), top, top)


def halo_row(ref, k, x):
    return ref[k, pl.ds(x, 1), :]


def second_inner(
    post_ref, flag_ref, rate_ref, halo_ref, halo_flag,
    next_hbm, sums_ref, side_ref, edge_ref, next_ref, sems,
):
    width, length = rate_ref.shape[:2]
    groups = length // 8

    def keep(x):
        return pltpu.make_async_copy(next_ref.at[:, x], next_hbm.at[:, x], sems.at[x])

    def plane(x, carry):
        flux, count = carry
        for g in range(groups):
            local = [post_ref[q, x, tile(g), :] for q in range(19)]
            fluid = flag_ref[1, x, tile(g), :]

            def load(q, cx, cy):
                return shifted(
                    lambda at: post_ref[q, x - cx, at, :], g, groups, cy,
                    lambda: side_row(halo_ref, x - cx, q),
                    lambda: side_row(halo_ref, x - cx, q),
                )

            def load_flag(cz, cx, cy):
                return shifted(
                    lambda at: flag_ref[cz + 1, x - cx, at, :], g, groups, cy,
                    lambda: halo_row(halo_flag, (cz + 1) * 2, x - cx),
                    lambda: halo_row(halo_flag, (cz + 1) * 2 + 1, x - cx),
                )

            f, links = pull(local, load, open_by_flag(load_flag, fluid))
            post, mz = collide(f, rate_ref[x, tile(g), :])
            for q in range(19):
                next_ref[q, x, tile(g), :] = post[q]
            flux = flux + link_flux(post, links, mz, fluid)
            count = count + fluid
        keep(x).start()
        return flux, count

    zero = jnp.zeros((8, 128), F32)
    flux, count = lax.fori_loop(1, width - 1, plane, (zero, zero))
    sums_ref[0] = flux
    sums_ref[1] = count
    pitch = next_ref.shape[2]
    flat = next_ref.reshape(19, width * pitch, 128)
    for g in range(width // 8):
        low_at = pl.ds(g * 8 * pitch, 8, stride=pitch)
        high_at = pl.ds(g * 8 * pitch + length - 1, 8, stride=pitch)
        for k in range(5):
            side_ref[k, tile(g), :] = flat[DOWN_Y[k], low_at, :]
            side_ref[5 + k, tile(g), :] = flat[UP_Y[k], high_at, :]
    for s, x in enumerate((1, width - 2)):
        for g in range(groups):
            for q in range(19):
                edge_ref[q, s, tile(g), :] = next_ref[q, x, tile(g), :]

    def finish(x, carry):
        keep(x).wait()
        return carry

    lax.fori_loop(1, width - 1, finish, 0)


def second_faces(
    post_ref, flag_ref, rate_ref, halo_ref, halo_flag, sums_ref, side_ref, far_ref, near_ref,
    side_far, side_near, end_far, end_near, ends_ref, ends_copy, open_ref, share_ref,
):
    odd_x = parity("bx")
    odd_y = parity("by")
    length = rate_ref.shape[1]
    width = side_ref.shape[1]
    groups = length // 8
    flux = sums_ref[0]
    count = sums_ref[1]
    for s, side in enumerate((1, -1)):
        plane_at = 0 if s == 0 else width - 1
        group = UP_X if side == 1 else DOWN_X
        own = 0 if s == 0 else 3

        def came(k, at):
            far = far_ref[k, at, :]
            near = near_ref[k, at, :]
            if side == 1:
                return jnp.where(odd_x == 0, far, near)
            return jnp.where(odd_x == 0, near, far)

        for g in range(groups):
            local = [post_ref[q, own, tile(g), :] for q in range(19)]
            fluid = flag_ref[1, own, tile(g), :]

            def load(q, cx, cy):
                if cx == side:
                    return came(group.index(q), pl.ds(1 + g * 8 - cy, 8))
                return shifted(
                    lambda at: post_ref[q, own - cx, at, :], g, groups, cy,
                    lambda: side_row(halo_ref, plane_at - cx, q),
                    lambda: side_row(halo_ref, plane_at - cx, q),
                )

            def load_flag(cz, cx, cy):
                if cx == side:
                    return turn(came(5, pl.ds(1 + g * 8 - cy, 8)), cz)
                return shifted(
                    lambda at: flag_ref[cz + 1, own - cx, at, :], g, groups, cy,
                    lambda: halo_row(halo_flag, (cz + 1) * 2, plane_at - cx),
                    lambda: halo_row(halo_flag, (cz + 1) * 2 + 1, plane_at - cx),
                )

            f, links = pull(local, load, open_by_flag(load_flag, fluid))
            post, mz = collide(f, rate_ref[s, tile(g), :])
            for q in range(19):
                ends_ref[q, s, tile(g), :] = post[q]
                ends_copy[q, s, tile(g), :] = post[q]
                if q:
                    open_ref[q - 1, s, tile(g), :] = jnp.where(links[q], 1.0, 0.0)
            flux = flux + link_flux(post, links, mz, fluid)
            count = count + fluid

    for k in range(5):
        for g in range(groups):
            low = ends_ref[DOWN_X[k], 0, tile(g), :]
            high = ends_ref[UP_X[k], 1, tile(g), :]
            end_far[k, tile(g), :] = jnp.where(odd_x == 0, low, high)
            end_near[k, tile(g), :] = jnp.where(odd_x == 0, high, low)
    for k in range(5):
        for g in range(width // 8):
            low = side_ref[k, tile(g), :]
            high = side_ref[5 + k, tile(g), :]
            side_far[k, tile(g), :] = jnp.where(odd_y == 0, low, high)
            side_near[k, tile(g), :] = jnp.where(odd_y == 0, high, low)
        for s, x in enumerate((0, width - 1)):
            low = ends_ref[DOWN_Y[k], s, pl.ds(0, 1), :]
            high = ends_ref[UP_Y[k], s, pl.ds(length - 1, 1), :]
            side_far[k, pl.ds(x, 1), :] = jnp.where(odd_y == 0, low, high)
            side_near[k, pl.ds(x, 1), :] = jnp.where(odd_y == 0, high, low)
    lane = lax.broadcasted_iota(jnp.int32, (1, 128), 1)
    total = jnp.sum(jnp.sum(flux, axis=0, keepdims=True), axis=1, keepdims=True)
    cells = jnp.sum(jnp.sum(count, axis=0, keepdims=True), axis=1, keepdims=True)
    row = jnp.where(lane < 64, total, cells)
    share_ref[...] = jnp.broadcast_to(row[None], share_ref.shape)
    for k, (q, dx, dy) in enumerate(CORNERS):
        y = length - 1 if dy == 1 else 0
        share_ref[device_at(dx, dy), 1, :] = ends_ref[q, 1 if dx == 1 else 0, y, :]


def last_inner(
    next_hbm, flag_hbm, ends_ref, halo_flag, far_ref, near_ref,
    out_hbm, halo_out, halo_ref, next_ref, flag_ref, out_buf, in_sems, flag_sem, sems,
):
    odd_y = parity("by")
    width, length = out_hbm.shape[1:3]
    groups = length // 8
    slots = out_buf.shape[0]
    ahead = 8

    def fetch(x):
        return pltpu.make_async_copy(next_hbm.at[:, x], next_ref.at[:, x], in_sems.at[x])

    for x in range(1, 3):
        fetch(x).start()
    get_flags = pltpu.make_async_copy(flag_hbm, flag_ref, flag_sem)
    get_flags.start()
    for x in range(3, 1 + ahead):
        fetch(x).start()
    for k in range(5):
        for g in range(width // 8):
            far = far_ref[k, tile(g), :]
            near = near_ref[k, tile(g), :]
            for out_ref in (halo_ref, halo_out):
                out_ref[k, tile(g), :] = jnp.where(odd_y == 0, far, near)
                out_ref[5 + k, tile(g), :] = jnp.where(odd_y == 0, near, far)

    def copy_out(x):
        slot = lax.rem(x, slots)
        return pltpu.make_async_copy(out_buf.at[slot], out_hbm.at[:, x], sems.at[slot])

    def one_plane(x, special):
        slot = lax.rem(x, slots)
        if special >= 0:
            fetch(x + 1).wait()

        @pl.when(x + ahead < width - 1)
        def _():
            fetch(x + ahead).start()

        @pl.when(x > slots)
        def _():
            copy_out(x - slots).wait()

        for g in range(groups):
            local = [next_ref[q, x, tile(g), :] for q in range(19)]

            def load(q, cx, cy):
                def read(at):
                    if special == cx and cx != 0:
                        return ends_ref[q, 0 if cx == 1 else 1, at, :]
                    return next_ref[q, x - cx, at, :]

                return shifted(
                    read, g, groups, cy,
                    lambda: side_row(halo_ref, x - cx, q),
                    lambda: side_row(halo_ref, x - cx, q),
                )

            def load_flag(cz, cx, cy):
                return shifted(
                    lambda at: flag_ref[cz + 1, x - cx, at, :], g, groups, cy,
                    lambda: halo_row(halo_flag, (cz + 1) * 2, x - cx),
                    lambda: halo_row(halo_flag, (cz + 1) * 2 + 1, x - cx),
                )

            f, _ = pull(local, load, open_by_flag(load_flag, flag_ref[1, x, tile(g), :]))
            for q in range(19):
                out_buf[slot, q, tile(g), :] = f[q]
        copy_out(x).start()

    def plane(x, carry):
        one_plane(x, 0)
        return carry

    get_flags.wait()
    fetch(1).wait()
    one_plane(1, 1)
    lax.fori_loop(2, width - 2, plane, 0)
    one_plane(width - 2, -1)

    def finish(x, carry):
        copy_out(x).wait()
        return carry

    lax.fori_loop(width - 1 - slots, width - 1, finish, 0)


def last_faces(
    out_in, ends_ref, edge_ref, open_ref, halo_ref, far_ref, near_ref, share_ref,
    out_hbm, mean_ref, came_ref, out_buf, sems,
):
    del out_in
    odd_x = parity("bx")
    width, length = out_hbm.shape[1:3]
    groups = length // 8
    copies = []
    for s, side in enumerate((1, -1)):
        group = UP_X if side == 1 else DOWN_X
        plane_at = 0 if s == 0 else width - 1
        for k in range(5):
            for g in range(groups):
                far = far_ref[k, tile(g), :]
                near = near_ref[k, tile(g), :]
                if side == 1:
                    came_ref[s, k, pl.ds(OFF + g * 8, 8), :] = jnp.where(odd_x == 0, far, near)
                else:
                    came_ref[s, k, pl.ds(OFF + g * 8, 8), :] = jnp.where(odd_x == 0, near, far)
        for k, (q, dx, dy) in enumerate(CORNERS):
            if dx == side:
                y = OFF - 1 if dy == 1 else OFF + length
                came_ref[s, group.index(q), y, :] = share_ref[device_at(-dx, -dy), 1, :]
        for g in range(groups):
            local = [ends_ref[q, s, tile(g), :] for q in range(19)]

            def load(q, cx, cy):
                if cx == side:
                    return came_ref[s, group.index(q), pl.ds(OFF + g * 8 - cy, 8), :]
                source = ends_ref if cx == 0 else edge_ref
                return shifted(
                    lambda at: source[q, s, at, :], g, groups, cy,
                    lambda: side_row(halo_ref, plane_at - cx, q),
                    lambda: side_row(halo_ref, plane_at - cx, q),
                )

            f, _ = pull(local, load, lambda q: open_ref[q - 1, s, tile(g), :] > 0.5)
            for q in range(19):
                out_buf[s, q, tile(g), :] = f[q]
        copies.append(pltpu.make_async_copy(out_buf.at[s], out_hbm.at[:, plane_at], sems.at[s]))
        copies[s].start()
    total = jnp.sum(share_ref[:, 0, :], axis=0, keepdims=True)
    lane = lax.broadcasted_iota(jnp.int32, (1, 128), 1)
    flux = jnp.sum(jnp.where(lane == 0, total, 0.0), axis=1, keepdims=True)
    cells = jnp.sum(jnp.where(lane == 127, total, 0.0), axis=1, keepdims=True)
    mean_ref[...] = jnp.broadcast_to(flux / cells, mean_ref.shape)
    for copy in copies:
        copy.wait()


def whole(count=1):
    return [pl.BlockSpec(memory_space=pltpu.VMEM)] * count


def anywhere(count=1):
    return [pl.BlockSpec(memory_space=pl.ANY)] * count


def vmem(*shape):
    return pltpu.VMEM(shape, F32)


def held(*arrays):
    return [pltpu.with_memory_space_constraint(a, pltpu.VMEM) for a in arrays]


def main_memory(*arrays):
    return [pltpu.with_memory_space_constraint(a, pltpu.HBM) for a in arrays]


def call(kernel, scratch_mib, **kwargs):
    return pl.pallas_call(
        kernel,
        compiler_params=pltpu.CompilerParams(vmem_limit_bytes=scratch_mib * MIB),
        name=kernel.__name__,
        **kwargs,
    )


def pairs_of(count):
    far = [(i, (i + 1) % count if i % 2 else (i - 1) % count) for i in range(count)]
    near = [(i, i ^ 1) for i in range(count)]
    return far, near


def exchange(far, near, axis):
    far_pairs, near_pairs = pairs_of(lax.axis_size(axis))
    return lax.ppermute(far, axis, far_pairs), lax.ppermute(near, axis, near_pairs)


def body(populations, fluid_mask, rate_class, class_rates):
    width, length, depth = fluid_mask.shape
    count = lax.axis_size("bx") * lax.axis_size("by")
    given = main_memory(populations, fluid_mask, rate_class, class_rates)

    far, near = call(
        first_faces,
        7,
        in_specs=anywhere(4),
        out_specs=whole(2),
        out_shape=[vmem(6, width, depth)] * 2,
        scratch_shapes=[
            pltpu.VMEM((2, 19, width, 1, depth), F32),
            pltpu.VMEM((2, width, 1, depth), jnp.int32),
            pltpu.VMEM((2, width, 1, depth), jnp.int32),
            pltpu.SMEM((4,), F32),
            pltpu.SemaphoreType.DMA((2, 3)),
            pltpu.SemaphoreType.DMA,
        ],
    )(*given)
    got_far, got_near = exchange(far, near, "by")

    post, flag, flag_last, rate, edge, edge_flag, edge_rate, face = call(
        first_step,
        13,
        in_specs=anywhere(5),
        out_specs=whole(2) + anywhere(1) + whole(5),
        out_shape=[
            vmem(19, width, length, depth),
            vmem(3, width, length, depth),
            pltpu.HBM((3, width, length, depth), F32),
            vmem(width, length, depth),
            vmem(19, 4, length, depth),
            vmem(3, 4, length, depth),
            vmem(2, length, depth),
            vmem(12, length, depth),
        ],
        scratch_shapes=[
            pltpu.VMEM((19, width, length, depth), F32),
            pltpu.VMEM((width, length, depth), jnp.int32),
            pltpu.VMEM((width, length, depth), jnp.int32),
            pltpu.SMEM((4,), F32),
            pltpu.SemaphoreType.DMA((16,)),
            pltpu.SemaphoreType.DMA((3,)),
            pltpu.SemaphoreType.DMA((16,)),
        ],
    )(*given, far)

    far, near, halo, halo_flag, halo_edge, halo_flag_edge, halo_flag_last = call(
        join_sides,
        2,
        in_specs=whole(3),
        out_specs=whole(7),
        out_shape=[vmem(6, length + 8, depth)] * 2
        + [vmem(10, width, depth), vmem(6, width, depth)] * 2
        + [vmem(6, width, depth)],
    )(*held(face, got_far, got_near))
    got_far, got_near = exchange(far, near, "bx")

    after, sums, side, after_edge = call(
        second_inner,
        12,
        in_specs=whole(5),
        out_specs=anywhere(1) + whole(3),
        out_shape=[
            pltpu.HBM(populations.shape, F32),
            vmem(2, 8, depth),
            vmem(10, width, depth),
            vmem(19, 2, length, depth),
        ],
        scratch_shapes=[
            pltpu.VMEM((19, width, length, depth), F32),
            pltpu.SemaphoreType.DMA((width,)),
        ],
    )(*held(post, flag, rate, halo, halo_flag))

    side_far, side_near, end_far, end_near, ends, ends_copy, open_links, share = call(
        second_faces,
        2,
        in_specs=whole(9),
        out_specs=whole(8),
        out_shape=[vmem(5, width, depth)] * 2
        + [vmem(5, length, depth)] * 2
        + [vmem(19, 2, length, depth)] * 2
        + [vmem(18, 2, length, depth), vmem(count, 2, depth)],
    )(*held(edge, edge_flag, edge_rate, halo_edge, halo_flag_edge, sums, side, got_far, got_near))
    side_far, side_near = exchange(side_far, side_near, "by")
    end_far, end_near = exchange(end_far, end_near, "bx")
    share = lax.all_to_all(share, ("bx", "by"), 0, 0)

    final, halo = call(
        last_inner,
        17,
        in_specs=anywhere(2) + whole(4),
        out_specs=anywhere(1) + whole(1),
        out_shape=[pltpu.HBM(populations.shape, F32), vmem(10, width, depth)],
        scratch_shapes=[
            pltpu.VMEM((10, width, depth), F32),
            pltpu.VMEM((19, width, length, depth), F32),
            pltpu.VMEM((3, width, length, depth), F32),
            pltpu.VMEM((12, 19, length, depth), F32),
            pltpu.SemaphoreType.DMA((width,)),
            pltpu.SemaphoreType.DMA,
            pltpu.SemaphoreType.DMA((12,)),
        ],
    )(*main_memory(after, flag_last), *held(ends, halo_flag_last, side_far, side_near))

    final, mean = call(
        last_faces,
        3,
        in_specs=anywhere(1) + whole(7),
        out_specs=anywhere(1) + whole(1),
        out_shape=[
            pltpu.HBM(populations.shape, F32),
            jax.ShapeDtypeStruct((1, depth), F32),
        ],
        scratch_shapes=[
            pltpu.VMEM((2, 5, length + 2 * OFF, depth), F32),
            pltpu.VMEM((2, 19, length, depth), F32),
            pltpu.SemaphoreType.DMA((2,)),
        ],
        input_output_aliases={0: 0},
    )(*main_memory(final), *held(ends_copy, after_edge, open_links, halo, end_far, end_near, share))
    return final, mean[0, :1]


def solution(mesh):
    placed = (P(None, "bx", "by", None), P("bx", "by", None), P("bx", "by", None), P())
    return jax.shard_map(
        body,
        mesh=mesh,
        in_specs=placed,
        out_specs=(P(None, "bx", "by", None), P()),
        check_vma=False,
    )
```

```python
import jax
import jax.numpy as jnp
from jax import lax
from jax.experimental import pallas as pl
from jax.experimental.pallas import tpu as pltpu
from jax.sharding import PartitionSpec as P

VELOCITY = [
    (0, 0, 0),
    (1, 0, 0),
    (-1, 0, 0),
    (0, 1, 0),
    (0, -1, 0),
    (0, 0, 1),
    (0, 0, -1),
    (1, 1, 0),
    (-1, -1, 0),
    (1, -1, 0),
    (-1, 1, 0),
    (1, 0, 1),
    (-1, 0, -1),
    (1, 0, -1),
    (-1, 0, 1),
    (0, 1, 1),
    (0, -1, -1),
    (0, 1, -1),
    (0, -1, 1),
]
OPPOSITE = [0, 2, 1, 4, 3, 6, 5, 8, 7, 10, 9, 12, 11, 14, 13, 16, 15, 18, 17]
UP_X = [q for q in range(19) if VELOCITY[q][0] == 1]
DOWN_X = [OPPOSITE[q] for q in UP_X]
UP_Y = [q for q in range(19) if VELOCITY[q][1] == 1]
DOWN_Y = [OPPOSITE[q] for q in UP_Y]
CORNERS = [(7, 1, 1), (8, -1, -1), (9, 1, -1), (10, -1, 1)]

OFF = 8
F32 = jnp.float32
MIB = 1024 * 1024


def collide(f, rate):
    plus = {}
    diff = {}
    for q in range(1, 19, 2):
        plus[q] = f[q] + f[q + 1]
        diff[q] = f[q] - f[q + 1]
    rho = ((f[0] + plus[1]) + (plus[3] + plus[5])) + (
        ((plus[7] + plus[9]) + (plus[11] + plus[13])) + (plus[15] + plus[17])
    )
    mx = (diff[1] + diff[7]) + (diff[9] + diff[11]) + diff[13]
    my = (diff[3] + diff[7]) + (diff[15] - diff[9]) + diff[17]
    mz = (diff[5] + diff[11]) + (diff[15] - diff[13]) - diff[17]
    inv = 4.5 / rho
    ux = inv * mx
    uy = inv * my
    uz = inv * mz
    tx = ux * mx
    ty = uy * my
    tz = uz * mz
    base = rho - ((tx + ty) + tz) * (1.0 / 3.0)
    keep = 1.0 - rate
    r36 = rate * (1.0 / 36.0)
    r18 = rate * (1.0 / 18.0)
    r12 = rate * (1.0 / 12.0)
    gx = r12 * mx
    gy = r12 * my
    gz = r12 * mz
    ux2 = ux + ux
    uy2 = uy + uy
    cross = {7: ux2 * my, 11: ux2 * mz, 15: uy2 * mz}
    pair_base = {7: base + (tx + ty), 11: base + (tx + tz), 15: base + (ty + tz)}
    lean = {7: (gx, gy), 11: (gx, gz), 15: (gy, gz)}
    out = [None] * 19
    out[0] = keep * f[0] + (rate * (1.0 / 3.0)) * base
    for q, t, g in ((1, tx, gx), (3, ty, gy), (5, tz, gz)):
        even = r18 * (base + t)
        odd = g + g
        out[q] = keep * f[q] + (even + odd)
        out[q + 1] = keep * f[q + 1] + (even - odd)
    for q in (7, 11, 15):
        one, two = lean[q]
        even = r36 * (pair_base[q] + cross[q])
        odd = one + two
        out[q] = keep * f[q] + (even + odd)
        out[q + 1] = keep * f[q + 1] + (even - odd)
        even = r36 * (pair_base[q] - cross[q])
        odd = one - two
        out[q + 2] = keep * f[q + 2] + (even + odd)
        out[q + 3] = keep * f[q + 3] + (even - odd)
    return out, mz


def turn(value, step):
    if step == 0:
        return value
    return pltpu.roll(value, step % value.shape[-1], axis=value.ndim - 1)


def cell_rate(cls, fluid, rates):
    rate = jnp.where(cls == 0, rates[0], rates[1])
    rate = jnp.where(cls == 2, rates[2], rate)
    rate = jnp.where(cls == 3, rates[3], rate)
    return jnp.where(fluid, rate, 0.0)


def pull(local, load, is_open):
    out = [local[0]]
    links = [None]
    for q in range(1, 19):
        move = VELOCITY[q]
        source = local[q] if move[0] == 0 and move[1] == 0 else load(q, move[0], move[1])
        links.append(is_open(q))
        out.append(jnp.where(links[q], turn(source, move[2]), local[OPPOSITE[q]]))
    return out, links


def open_by_flag(load_flag, fluid):
    limit = jnp.where(fluid > 0.5, 0.5, 2.0)

    def is_open(q):
        move = VELOCITY[q]
        return load_flag(move[2], move[0], move[1]) > limit

    return is_open


def link_flux(post, links, mz, fluid):
    total = None
    for q in range(19):
        step = VELOCITY[q][2]
        if step == 0:
            continue
        term = jnp.where(links[OPPOSITE[q]], post[q], 0.0)
        if total is None:
            total = term if step > 0 else -term
        else:
            total = total + term if step > 0 else total - term
    return (total + total) - jnp.where(fluid > 0.5, mz, 0.0)


def beyond(ref, k, plane, g, cy, spare):
    length = ref.shape[2]
    if not spare:
        return pltpu.roll(ref[k, plane, tile(g), :], cy % 8, axis=0)
    flat = ref.reshape(ref.shape[0], ref.shape[1] * length, ref.shape[3])
    return flat[k, pl.ds(plane * length + (g * 8 - cy), 8), :]


def shifted(ref, k, plane, g, cy, low=None, high=None, spare=False):
    groups = ref.shape[2] // 8
    if cy == 1 and g == 0:
        value = beyond(ref, k, plane, g, cy, spare)
        if low is None:
            return value
        return jnp.where(lax.broadcasted_iota(jnp.int32, value.shape, 0) == 0, low(), value)
    if cy == -1 and g == groups - 1:
        value = beyond(ref, k, plane, g, cy, spare)
        if high is None:
            return value
        return jnp.where(lax.broadcasted_iota(jnp.int32, value.shape, 0) == 7, high(), value)
    return ref[k, plane, pl.ds(g * 8 - cy, 8), :]


def side_row(halo_ref, x, q):
    k = UP_Y.index(q) if q in UP_Y else 5 + DOWN_Y.index(q)
    return halo_ref[k, pl.ds(x, 1), :]


def tile(g):
    return pl.ds(g * 8, 8)


def parity(axis):
    return lax.rem(lax.axis_index(axis), 2)


def device_at(dx, dy):
    size_x = lax.axis_size("bx")
    size_y = lax.axis_size("by")
    at_x = lax.rem(lax.axis_index("bx") + (dx + size_x), size_x)
    at_y = lax.rem(lax.axis_index("by") + (dy + size_y), size_y)
    return at_x * size_y + at_y


def first_faces(
    f_hbm, mask_hbm, cls_hbm, rates_hbm, far_ref, near_ref,
    f_buf, mask_buf, cls_buf, rates_ref, sems, rates_sem,
):
    odd = parity("by")
    width = f_hbm.shape[1]
    length = f_hbm.shape[2]
    get_rates = pltpu.make_async_copy(rates_hbm, rates_ref, rates_sem)
    get_rates.start()
    copies = []
    for side in range(2):
        src = pl.ds(side * (length - 1), 1)
        group = [
            pltpu.make_async_copy(f_hbm.at[:, :, src, :], f_buf.at[side], sems.at[side, 0]),
            pltpu.make_async_copy(mask_hbm.at[:, src, :], mask_buf.at[side], sems.at[side, 1]),
            pltpu.make_async_copy(cls_hbm.at[:, src, :], cls_buf.at[side], sems.at[side, 2]),
        ]
        for copy in group:
            copy.start()
        copies.append(group)
    get_rates.wait()
    rates = [rates_ref[k] for k in range(4)]
    leaving = []
    for side in range(2):
        for copy in copies[side]:
            copy.wait()
        f_rows = f_buf.at[side].reshape(19, width, 128)
        mask_rows = mask_buf.at[side].reshape(width, 128)
        cls_rows = cls_buf.at[side].reshape(width, 128)
        for g in range(width // 8):
            fluid = mask_rows[tile(g), :] == 1
            rate = cell_rate(cls_rows[tile(g), :], fluid, rates)
            post, _ = collide([f_rows[q, tile(g), :] for q in range(19)], rate)
            values = [post[q] for q in (UP_Y if side else DOWN_Y)]
            leaving.append(values + [jnp.where(fluid, 1.0, 0.0)])
    for g in range(width // 8):
        for k in range(6):
            low = leaving[g][k]
            high = leaving[width // 8 + g][k]
            far_ref[k, tile(g), :] = jnp.where(odd == 0, low, high)
            near_ref[k, tile(g), :] = jnp.where(odd == 0, high, low)


def first_step(
    f_ref, mask_ref, cls_ref, rates_hbm, order_ref,
    post_ref, flag_ref, rate_ref, edge_ref, edge_flag, edge_rate, face_ref,
    rates_ref, rates_sem,
):
    del order_ref
    width, length = mask_ref.shape[:2]
    groups = length // 8
    get_rates = pltpu.make_async_copy(rates_hbm, rates_ref, rates_sem)
    get_rates.start()
    get_rates.wait()
    rates = [rates_ref[k] for k in range(4)]

    def plane(x, carry):
        for g in range(groups):
            fluid = mask_ref[x, tile(g), :] == 1
            rate = cell_rate(cls_ref[x, tile(g), :], fluid, rates)
            post, _ = collide([f_ref[q, x, tile(g), :] for q in range(19)], rate)
            for q in range(19):
                post_ref[q, x + 1, tile(g), :] = post[q]
            rate_ref[x, tile(g), :] = rate
            flag = jnp.where(fluid, 1.0, 0.0)
            for step in (-1, 0, 1):
                flag_ref[step + 1, x + 1, tile(g), :] = turn(flag, step)
        return carry

    lax.fori_loop(0, width, plane, 0)
    for e, x in enumerate((0, 1, width - 2, width - 1)):
        for g in range(groups):
            for q in range(19):
                edge_ref[q, e, tile(g), :] = post_ref[q, x + 1, tile(g), :]
            for s in range(3):
                edge_flag[s, e, tile(g), :] = flag_ref[s, x + 1, tile(g), :]
    for s, x in enumerate((0, width - 1)):
        leaving = UP_X if s else DOWN_X
        for g in range(groups):
            edge_rate[s, tile(g), :] = rate_ref[x, tile(g), :]
            for k in range(5):
                face_ref[s * 6 + k, tile(g), :] = post_ref[leaving[k], x + 1, tile(g), :]
            face_ref[s * 6 + 5, tile(g), :] = flag_ref[1, x + 1, tile(g), :]


def join_sides(
    face_ref, far_ref, near_ref,
    far_out, near_out, halo_ref, flag_ref, halo_edge, flag_edge, flag_last,
):
    odd_x = parity("bx")
    odd_y = parity("by")
    width = far_ref.shape[1]
    length = face_ref.shape[1]
    for g in range(width // 8):
        for k in range(6):
            far = far_ref[k, tile(g), :]
            near = near_ref[k, tile(g), :]
            low = jnp.where(odd_y == 0, far, near)
            high = jnp.where(odd_y == 0, near, far)
            if k < 5:
                for out_ref in (halo_ref, halo_edge):
                    out_ref[k, tile(g), :] = low
                    out_ref[5 + k, tile(g), :] = high
                continue
            for step in (-1, 0, 1):
                for side, value in enumerate((low, high)):
                    turned = turn(value, step)
                    for out_ref in (flag_ref, flag_edge, flag_last):
                        out_ref[(step + 1) * 2 + side, tile(g), :] = turned
    def put(k, at, low, high):
        far_out[k, at, :] = jnp.where(odd_x == 0, low, high)
        near_out[k, at, :] = jnp.where(odd_x == 0, high, low)

    for k in range(6):
        for g in range(length // 8):
            put(k, pl.ds(1 + g * 8, 8), face_ref[k, tile(g), :], face_ref[6 + k, tile(g), :])
        if k == 5:
            for side in range(2):
                ends = [halo_row(flag_ref, 2 + side, x) for x in (0, width - 1)]
                put(k, pl.ds(side * (length + 1), 1), *ends)
            continue
        q = DOWN_X[k]
        if q in UP_Y:
            bottom, top = side_row(halo_ref, 0, q), side_row(halo_ref, width - 1, OPPOSITE[q])
        elif q in DOWN_Y:
            bottom, top = side_row(halo_ref, width - 1, OPPOSITE[q]), side_row(halo_ref, 0, q)
        else:
            continue
        put(k, pl.ds(0, 1), bottom, bottom)
        put(k, pl.ds(length + 1, 1), top, top)


def halo_row(ref, k, x):
    return ref[k, pl.ds(x, 1), :]


def second_inner(
    post_ref, flag_ref, rate_ref, halo_ref, halo_flag,
    out_hbm, sums_ref, side_ref, side_copy, own_flag, edge_ref, edge_flag,
    next_ref, out_buf, sems,
):
    width, length = rate_ref.shape[:2]
    groups = length // 8
    chunk = out_buf.shape[2]
    slots = out_buf.shape[0]

    def collide_tile(x, g, carry):
        flux, count = carry
        local = [post_ref[q, x + 1, tile(g), :] for q in range(19)]
        fluid = flag_ref[1, x + 1, tile(g), :]

        def load(q, cx, cy):
            def side():
                return side_row(halo_ref, x - cx, q)

            return shifted(post_ref, q, x + 1 - cx, g, cy, side, side, spare=True)

        def load_flag(cz, cx, cy):
            return shifted(
                flag_ref, cz + 1, x + 1 - cx, g, cy,
                lambda: halo_row(halo_flag, (cz + 1) * 2, x - cx),
                lambda: halo_row(halo_flag, (cz + 1) * 2 + 1, x - cx),
                spare=True,
            )

        f, links = pull(local, load, open_by_flag(load_flag, fluid))
        post, mz = collide(f, rate_ref[x, tile(g), :])
        for q in range(19):
            next_ref[q, x, tile(g), :] = post[q]
        flux = flux + link_flux(post, links, mz, fluid)
        count = count + fluid
        return flux, count

    def stream_tile(x, g, slot, j):
        local = [next_ref[q, x, tile(g), :] for q in range(19)]

        def load(q, cx, cy):
            return shifted(next_ref, q, x - cx, g, cy, spare=True)

        def load_flag(cz, cx, cy):
            return shifted(flag_ref, cz + 1, x + 1 - cx, g, cy, spare=True)

        f, _ = pull(local, load, open_by_flag(load_flag, flag_ref[1, x + 1, tile(g), :]))
        for q in range(19):
            out_buf[slot, q, j, tile(g), :] = f[q]

    def copy_out(c):
        slot = lax.rem(c, slots)
        return pltpu.make_async_copy(
            out_buf.at[slot], out_hbm.at[:, pl.ds(2 + c * chunk, chunk)], sems.at[slot]
        )

    def first(x, carry):
        for g in range(groups):
            carry = collide_tile(x, g, carry)
        return carry

    zero = jnp.zeros((8, 128), F32)
    carry = lax.fori_loop(1, 4, first, (zero, zero))
    parts = (width - 4) // chunk

    def part(c, carry, steps=chunk):
        slot = lax.rem(c, slots)

        @pl.when(c >= slots)
        def _():
            copy_out(c - slots).wait()

        def step(j, carry):
            x = 2 + c * chunk + j
            for g in range(groups):
                carry = collide_tile(x + 2, g, carry)
                stream_tile(x, g, slot, j)
            return carry

        carry = lax.fori_loop(0, steps, step, carry)
        for j in range(steps, chunk):
            for g in range(groups):
                stream_tile(2 + c * chunk + j, g, slot, j)
        copy_out(c).start()
        return carry

    carry = lax.fori_loop(0, parts - 1, part, carry)
    flux, count = part(parts - 1, carry, chunk - 1)
    sums_ref[0] = flux
    sums_ref[1] = count
    flat = next_ref.reshape(19, width * length, 128)
    flags = flag_ref.reshape(3, (width + 2) * length, 128)
    for g in range(width // 8):
        low_at = pl.ds(g * 8 * length, 8, stride=length)
        high_at = pl.ds(g * 8 * length + length - 1, 8, stride=length)
        for k in range(5):
            low = flat[DOWN_Y[k], low_at, :]
            high = flat[UP_Y[k], high_at, :]
            for to_ref in (side_ref, side_copy):
                to_ref[k, tile(g), :] = low
                to_ref[5 + k, tile(g), :] = high
        own_flag[0, tile(g), :] = flags[1, pl.ds((g * 8 + 1) * length, 8, stride=length), :]
        own_flag[1, tile(g), :] = flags[1, pl.ds((g * 8 + 2) * length - 1, 8, stride=length), :]
    for e, x in enumerate((1, 2, width - 3, width - 2)):
        for g in range(groups):
            for q in range(19):
                edge_ref[q, e, tile(g), :] = next_ref[q, x, tile(g), :]
    for e, x in enumerate((0, 1, 2, width - 3, width - 2, width - 1)):
        for g in range(groups):
            for s in range(3):
                edge_flag[s, e, tile(g), :] = flag_ref[s, x + 1, tile(g), :]
    for c in range(parts - slots, parts):
        copy_out(c).wait()


def second_faces(
    post_ref, flag_ref, rate_ref, halo_ref, halo_flag, sums_ref, side_ref, far_ref, near_ref,
    side_far, side_near, end_far, end_near, ends_ref, came_flag, share_ref,
):
    odd_x = parity("bx")
    odd_y = parity("by")
    length = rate_ref.shape[1]
    width = side_ref.shape[1]
    groups = length // 8
    flux = sums_ref[0]
    count = sums_ref[1]
    for s, side in enumerate((1, -1)):
        plane_at = 0 if s == 0 else width - 1
        group = UP_X if side == 1 else DOWN_X
        own = 0 if s == 0 else 3

        def came(k, at):
            far = far_ref[k, at, :]
            near = near_ref[k, at, :]
            if side == 1:
                return jnp.where(odd_x == 0, far, near)
            return jnp.where(odd_x == 0, near, far)

        for g in range(length // 8 + 1):
            value = came(5, tile(g))
            for step in (-1, 0, 1):
                came_flag[step + 1, s, tile(g), :] = turn(value, step)
        for g in range(groups):
            local = [post_ref[q, own, tile(g), :] for q in range(19)]
            fluid = flag_ref[1, own, tile(g), :]

            def load(q, cx, cy):
                def beside():
                    return side_row(halo_ref, plane_at - cx, q)

                if cx == side:
                    return came(group.index(q), pl.ds(1 + g * 8 - cy, 8))
                return shifted(post_ref, q, own - cx, g, cy, beside, beside)

            def load_flag(cz, cx, cy):
                if cx == side:
                    return came_flag[cz + 1, s, pl.ds(1 + g * 8 - cy, 8), :]
                return shifted(
                    flag_ref, cz + 1, own - cx, g, cy,
                    lambda: halo_row(halo_flag, (cz + 1) * 2, plane_at - cx),
                    lambda: halo_row(halo_flag, (cz + 1) * 2 + 1, plane_at - cx),
                )

            f, links = pull(local, load, open_by_flag(load_flag, fluid))
            post, mz = collide(f, rate_ref[s, tile(g), :])
            for q in range(19):
                ends_ref[q, s, tile(g), :] = post[q]
            flux = flux + link_flux(post, links, mz, fluid)
            count = count + fluid

    for k in range(5):
        for g in range(groups):
            low = ends_ref[DOWN_X[k], 0, tile(g), :]
            high = ends_ref[UP_X[k], 1, tile(g), :]
            end_far[k, tile(g), :] = jnp.where(odd_x == 0, low, high)
            end_near[k, tile(g), :] = jnp.where(odd_x == 0, high, low)
    for k in range(5):
        for g in range(width // 8):
            low = side_ref[k, tile(g), :]
            high = side_ref[5 + k, tile(g), :]
            side_far[k, tile(g), :] = jnp.where(odd_y == 0, low, high)
            side_near[k, tile(g), :] = jnp.where(odd_y == 0, high, low)
        for s, x in enumerate((0, width - 1)):
            low = ends_ref[DOWN_Y[k], s, pl.ds(0, 1), :]
            high = ends_ref[UP_Y[k], s, pl.ds(length - 1, 1), :]
            side_far[k, pl.ds(x, 1), :] = jnp.where(odd_y == 0, low, high)
            side_near[k, pl.ds(x, 1), :] = jnp.where(odd_y == 0, high, low)
    lane = lax.broadcasted_iota(jnp.int32, (1, 128), 1)
    total = jnp.sum(jnp.sum(flux, axis=0, keepdims=True), axis=1, keepdims=True)
    cells = jnp.sum(jnp.sum(count, axis=0, keepdims=True), axis=1, keepdims=True)
    row = jnp.where(lane < 64, total, cells)
    share_ref[...] = jnp.broadcast_to(row[None], share_ref.shape)
    for k, (q, dx, dy) in enumerate(CORNERS):
        y = length - 1 if dy == 1 else 0
        share_ref[device_at(dx, dy), 1, :] = ends_ref[q, 1 if dx == 1 else 0, y, :]


def last_faces(
    out_in, ends_ref, edge_ref, edge_flag, came_flag, halo_flag, side_ref, own_flag,
    side_far, side_near, far_ref, near_ref, share_ref,
    out_hbm, mean_ref, halo_ref, came_ref, out_buf, row_buf, sems, row_sems,
):
    del out_in
    odd_x = parity("bx")
    odd_y = parity("by")
    width, length = out_hbm.shape[1:3]
    groups = length // 8
    copies = []
    for k in range(5):
        for g in range(width // 8):
            far = side_far[k, tile(g), :]
            near = side_near[k, tile(g), :]
            halo_ref[k, tile(g), :] = jnp.where(odd_y == 0, far, near)
            halo_ref[5 + k, tile(g), :] = jnp.where(odd_y == 0, near, far)

    for side, group in enumerate((UP_Y, DOWN_Y)):
        for k, q in enumerate(group):
            cx, _, cz = VELOCITY[q]
            for x in (1, 9, 17, width - 9):
                fluid = own_flag[side, pl.ds(x, 8), :]
                limit = jnp.where(fluid > 0.5, 0.5, 2.0)
                is_open = halo_flag[(cz + 1) * 2 + side, pl.ds(x - cx, 8), :] > limit
                source = turn(halo_ref[side * 5 + k, pl.ds(x - cx, 8), :], cz)
                value = jnp.where(is_open, source, side_ref[side * 5 + k, pl.ds(x, 8), :])
                row_buf[side * 5 + k, pl.ds(x, 8), 0, :] = value
            planes = pl.ds(2, width - 4)
            copy = pltpu.make_async_copy(
                row_buf.at[side * 5 + k, planes],
                out_hbm.at[q, planes, pl.ds(side * (length - 1), 1), :],
                row_sems.at[side * 5 + k],
            )
            copy.start()
            copies.append(copy)

    for s, side in enumerate((1, -1)):
        group = UP_X if side == 1 else DOWN_X
        for k in range(5):
            for g in range(groups):
                far = far_ref[k, tile(g), :]
                near = near_ref[k, tile(g), :]
                if side == 1:
                    came_ref[s, k, pl.ds(OFF + g * 8, 8), :] = jnp.where(odd_x == 0, far, near)
                else:
                    came_ref[s, k, pl.ds(OFF + g * 8, 8), :] = jnp.where(odd_x == 0, near, far)
        for k, (q, dx, dy) in enumerate(CORNERS):
            if dx == side:
                y = OFF - 1 if dy == 1 else OFF + length
                came_ref[s, group.index(q), y, :] = share_ref[device_at(-dx, -dy), 1, :]
        for outer in (0, 1):
            plane_at = outer if s == 0 else width - 1 - outer
            for g in range(groups):

                def at(plane):
                    if plane == 0:
                        return ends_ref, s
                    return edge_ref, plane - 1 if s == 0 else 4 - plane

                own_ref, own = at(outer)
                local = [own_ref[q, own, tile(g), :] for q in range(19)]

                def load(q, cx, cy):
                    def beside():
                        return side_row(halo_ref, plane_at - cx, q)

                    plane = outer - cx * side
                    if plane < 0:
                        return came_ref[s, group.index(q), pl.ds(OFF + g * 8 - cy, 8), :]
                    ref, index = at(plane)
                    return shifted(ref, q, index, g, cy, beside, beside)

                def load_flag(cz, cx, cy):
                    plane = outer - cx * side
                    if plane < 0:
                        return came_flag[cz + 1, s, pl.ds(1 + g * 8 - cy, 8), :]
                    return shifted(
                        edge_flag, cz + 1, plane if s == 0 else 5 - plane, g, cy,
                        lambda: halo_row(halo_flag, (cz + 1) * 2, plane_at - cx),
                        lambda: halo_row(halo_flag, (cz + 1) * 2 + 1, plane_at - cx),
                    )

                fluid = edge_flag[1, outer if s == 0 else 5 - outer, tile(g), :]
                f, _ = pull(local, load, open_by_flag(load_flag, fluid))
                for q in range(19):
                    out_buf[s, q, outer if s == 0 else 1 - outer, tile(g), :] = f[q]
        planes = pl.ds(0 if s == 0 else width - 2, 2)
        copy = pltpu.make_async_copy(out_buf.at[s], out_hbm.at[:, planes], sems.at[s])
        copy.start()
        copies.append(copy)
    total = jnp.sum(share_ref[:, 0, :], axis=0, keepdims=True)
    lane = lax.broadcasted_iota(jnp.int32, (1, 128), 1)
    flux = jnp.sum(jnp.where(lane == 0, total, 0.0), axis=1, keepdims=True)
    cells = jnp.sum(jnp.where(lane == 127, total, 0.0), axis=1, keepdims=True)
    mean_ref[...] = jnp.broadcast_to(flux / cells, mean_ref.shape)
    for copy in copies:
        copy.wait()


def whole(count=1):
    return [pl.BlockSpec(memory_space=pltpu.VMEM)] * count


def anywhere(count=1):
    return [pl.BlockSpec(memory_space=pl.ANY)] * count


def vmem(*shape):
    return pltpu.VMEM(shape, F32)


def held(*arrays):
    return [pltpu.with_memory_space_constraint(a, pltpu.VMEM) for a in arrays]


def main_memory(*arrays):
    return [pltpu.with_memory_space_constraint(a, pltpu.HBM) for a in arrays]


def call(kernel, scratch_mib, kib=0, **kwargs):
    return pl.pallas_call(
        kernel,
        cost_estimate=pl.CostEstimate(flops=0, bytes_accessed=kib * 1024, transcendentals=0),
        compiler_params=pltpu.CompilerParams(vmem_limit_bytes=scratch_mib * MIB),
        name=kernel.__name__,
        **kwargs,
    )


def pairs_of(count):
    far = [(i, (i + 1) % count if i % 2 else (i - 1) % count) for i in range(count)]
    near = [(i, i ^ 1) for i in range(count)]
    return far, near


def exchange(far, near, axis):
    far_pairs, near_pairs = pairs_of(lax.axis_size(axis))
    return lax.ppermute(far, axis, far_pairs), lax.ppermute(near, axis, near_pairs)


def body(populations, fluid_mask, rate_class, class_rates):
    width, length, depth = fluid_mask.shape
    count = lax.axis_size("bx") * lax.axis_size("by")
    given = main_memory(populations, fluid_mask, rate_class, class_rates)

    far, near = call(
        first_faces,
        7,
        16384,
        in_specs=anywhere(4),
        out_specs=whole(2),
        out_shape=[vmem(6, width, depth)] * 2,
        scratch_shapes=[
            pltpu.VMEM((2, 19, width, 1, depth), F32),
            pltpu.VMEM((2, width, 1, depth), jnp.int32),
            pltpu.VMEM((2, width, 1, depth), jnp.int32),
            pltpu.SMEM((4,), F32),
            pltpu.SemaphoreType.DMA((2, 3)),
            pltpu.SemaphoreType.DMA,
        ],
    )(*given)
    got_far, got_near = exchange(far, near, "by")

    post, flag, rate, edge, edge_flag, edge_rate, face = call(
        first_step,
        2,
        in_specs=whole(3) + anywhere(2),
        out_specs=whole(7),
        out_shape=[
            vmem(19, width + 2, length, depth),
            vmem(3, width + 2, length, depth),
            vmem(width, length, depth),
            vmem(19, 4, length, depth),
            vmem(3, 4, length, depth),
            vmem(2, length, depth),
            vmem(12, length, depth),
        ],
        scratch_shapes=[pltpu.SMEM((4,), F32), pltpu.SemaphoreType.DMA],
    )(*held(populations, fluid_mask, rate_class), given[3], far)

    far, near, halo, halo_flag, halo_edge, halo_flag_edge, halo_flag_last = call(
        join_sides,
        2,
        in_specs=whole(3),
        out_specs=whole(7),
        out_shape=[vmem(6, length + 8, depth)] * 2
        + [vmem(10, width, depth), vmem(6, width, depth)] * 2
        + [vmem(6, width, depth)],
    )(*held(face, got_far, got_near))
    got_far, got_near = exchange(far, near, "bx")

    final, sums, side, side_copy, own_flag, after_edge, last_flag = call(
        second_inner,
        16,
        in_specs=whole(5),
        out_specs=anywhere(1) + whole(6),
        out_shape=[
            pltpu.HBM(populations.shape, F32),
            vmem(2, 8, depth),
            vmem(10, width, depth),
            vmem(10, width, depth),
            vmem(2, width, depth),
            vmem(19, 4, length, depth),
            vmem(3, 6, length, depth),
        ],
        scratch_shapes=[
            pltpu.VMEM((19, width, length, depth), F32),
            pltpu.VMEM((3, 19, 4, length, depth), F32),
            pltpu.SemaphoreType.DMA((3,)),
        ],
    )(*held(post, flag, rate, halo, halo_flag))

    side_far, side_near, end_far, end_near, ends, came_flag, share = call(
        second_faces,
        2,
        in_specs=whole(9),
        out_specs=whole(7),
        out_shape=[vmem(5, width, depth)] * 2
        + [vmem(5, length, depth)] * 2
        + [vmem(19, 2, length, depth), vmem(3, 2, length + 8, depth), vmem(count, 2, depth)],
    )(*held(edge, edge_flag, edge_rate, halo_edge, halo_flag_edge, sums, side, got_far, got_near))
    side_far, side_near = exchange(side_far, side_near, "by")
    end_far, end_near = exchange(end_far, end_near, "bx")
    share = lax.all_to_all(share, ("bx", "by"), 0, 0)

    final, mean = call(
        last_faces,
        6,
        in_specs=anywhere(1) + whole(12),
        out_specs=anywhere(1) + whole(1),
        out_shape=[
            pltpu.HBM(populations.shape, F32),
            jax.ShapeDtypeStruct((1, depth), F32),
        ],
        scratch_shapes=[
            pltpu.VMEM((10, width, depth), F32),
            pltpu.VMEM((2, 5, length + 2 * OFF, depth), F32),
            pltpu.VMEM((2, 19, 2, length, depth), F32),
            pltpu.VMEM((10, width, 1, depth), F32),
            pltpu.SemaphoreType.DMA((2,)),
            pltpu.SemaphoreType.DMA((10,)),
        ],
        input_output_aliases={0: 0},
    )(
        *main_memory(final),
        *held(ends, after_edge, last_flag, came_flag, halo_flag_last, side_copy, own_flag),
        *held(side_far, side_near, end_far, end_near, share),
    )
    return final, mean[0, :1]


def solution(mesh):
    placed = (P(None, "bx", "by", None), P("bx", "by", None), P("bx", "by", None), P())
    return jax.shard_map(
        body,
        mesh=mesh,
        in_specs=placed,
        out_specs=(P(None, "bx", "by", None), P()),
        check_vma=False,
    )
```

```python
import jax
import jax.numpy as jnp
from jax import lax
from jax.experimental import pallas as pl
from jax.experimental.pallas import tpu as pltpu
from jax.sharding import PartitionSpec as P

VELOCITY = [
    (0, 0, 0),
    (1, 0, 0),
    (-1, 0, 0),
    (0, 1, 0),
    (0, -1, 0),
    (0, 0, 1),
    (0, 0, -1),
    (1, 1, 0),
    (-1, -1, 0),
    (1, -1, 0),
    (-1, 1, 0),
    (1, 0, 1),
    (-1, 0, -1),
    (1, 0, -1),
    (-1, 0, 1),
    (0, 1, 1),
    (0, -1, -1),
    (0, 1, -1),
    (0, -1, 1),
]
OPPOSITE = [0, 2, 1, 4, 3, 6, 5, 8, 7, 10, 9, 12, 11, 14, 13, 16, 15, 18, 17]
UP_X = [q for q in range(19) if VELOCITY[q][0] == 1]
DOWN_X = [OPPOSITE[q] for q in UP_X]
UP_Y = [q for q in range(19) if VELOCITY[q][1] == 1]
DOWN_Y = [OPPOSITE[q] for q in UP_Y]
FLAG, NEXT, SUMS, RATE, ROWS = 5, 6, 11, 15, 16
F32 = jnp.float32
MIB = 1024 * 1024


def collide(f, rate):
    rho, mx, my, mz = moments(f)
    return relax(f, rho, mx, my, mz, rate), mz


def moments(f):
    plus = {}
    diff = {}
    for q in range(1, 19, 2):
        plus[q] = f[q] + f[q + 1]
        diff[q] = f[q] - f[q + 1]
    rho = ((f[0] + plus[1]) + (plus[3] + plus[5])) + (
        ((plus[7] + plus[9]) + (plus[11] + plus[13])) + (plus[15] + plus[17])
    )
    mx = (diff[1] + diff[7]) + (diff[9] + diff[11]) + diff[13]
    my = (diff[3] + diff[7]) + (diff[15] - diff[9]) + diff[17]
    mz = (diff[5] + diff[11]) + (diff[15] - diff[13]) - diff[17]
    return rho, mx, my, mz


def relax(f, rho, mx, my, mz, rate):
    inv = 4.5 / rho
    ux = inv * mx
    uy = inv * my
    uz = inv * mz
    tx = ux * mx
    ty = uy * my
    tz = uz * mz
    base = rho - ((tx + ty) + tz) * (1.0 / 3.0)
    keep = 1.0 - rate
    r36 = rate * (1.0 / 36.0)
    r18 = rate * (1.0 / 18.0)
    r12 = rate * (1.0 / 12.0)
    gx = r12 * mx
    gy = r12 * my
    gz = r12 * mz
    ux2 = ux + ux
    uy2 = uy + uy
    cross = {7: ux2 * my, 11: ux2 * mz, 15: uy2 * mz}
    pair_base = {7: base + (tx + ty), 11: base + (tx + tz), 15: base + (ty + tz)}
    lean = {7: (gx, gy), 11: (gx, gz), 15: (gy, gz)}
    out = [None] * 19

    def put(q, even, odd):
        if f[q] is not None:
            out[q] = keep * f[q] + (even + odd)
        if f[q + 1] is not None:
            out[q + 1] = keep * f[q + 1] + (even - odd)

    if f[0] is not None:
        out[0] = keep * f[0] + (rate * (1.0 / 3.0)) * base
    for q, t, g in ((1, tx, gx), (3, ty, gy), (5, tz, gz)):
        put(q, r18 * (base + t), g + g)
    for q in (7, 11, 15):
        one, two = lean[q]
        put(q, r36 * (pair_base[q] + cross[q]), one + two)
        put(q + 2, r36 * (pair_base[q] - cross[q]), one - two)
    return out


def turn(value, step):
    if step == 0:
        return value
    return pltpu.roll(value, step % value.shape[-1], axis=value.ndim - 1)


def cell_rate(cls, fluid, rates):
    rate = jnp.where(cls == 0, rates[0], rates[1])
    rate = jnp.where(cls == 2, rates[2], rate)
    rate = jnp.where(cls == 3, rates[3], rate)
    return jnp.where(fluid, rate, 0.0)


def pull(local, load, is_open):
    out = [local[0]]
    links = [None]
    for q in range(1, 19):
        links.append(is_open(q))
        out.append(jnp.where(links[q], load(q, *VELOCITY[q]), local[OPPOSITE[q]]))
    return out, links


def open_by_flag(load_flag, fluid):
    limit = jnp.where(fluid > 0.5, 0.5, 2.0)

    def is_open(q):
        move = VELOCITY[q]
        return load_flag(move[2], move[0], move[1]) > limit

    return is_open


def link_flux(post, links, mz, fluid):
    total = None
    for q in range(19):
        step = VELOCITY[q][2]
        if step == 0:
            continue
        term = jnp.where(links[OPPOSITE[q]], post[q], 0.0)
        if total is None:
            total = term if step > 0 else -term
        else:
            total = total + term if step > 0 else total - term
    return (total + total) - jnp.where(fluid > 0.5, mz, 0.0)


def beyond(ref, k, plane, g, cy, spare):
    length = ref.shape[2]
    if not spare:
        return pltpu.roll(ref[k, plane, tile(g), :], cy % 8, axis=0)
    flat = ref.reshape(ref.shape[0], ref.shape[1] * length, ref.shape[3])
    return flat[k, pl.ds(plane * length + (g * 8 - cy), 8), :]


def shifted(ref, k, plane, g, cy, low=None, high=None, spare=False, step=0):
    groups = ref.shape[2] // 8
    if cy == 1 and g == 0:
        value = beyond(ref, k, plane, g, cy, spare)
        if low is not None:
            value = jnp.where(lax.broadcasted_iota(jnp.int32, value.shape, 0) == 0, low(), value)
        return turn(value, step)
    if cy == -1 and g == groups - 1:
        value = beyond(ref, k, plane, g, cy, spare)
        if high is not None:
            value = jnp.where(lax.broadcasted_iota(jnp.int32, value.shape, 0) == 7, high(), value)
        return turn(value, step)
    return turn(ref[k, plane, pl.ds(g * 8 - cy, 8), :], step)


def side_row(halo_ref, x, q):
    if isinstance(x, int) and x < 0:
        x = 33
    k = UP_Y.index(q) if q in UP_Y else 5 + DOWN_Y.index(q)
    return halo_ref[k, pl.ds(x, 1), :]


def tile(g):
    return pl.ds(g * 8, 8)


def parity(axis):
    return lax.rem(lax.axis_index(axis), 2)


def first_faces(
    f_hbm, mask_hbm, cls_hbm, rates_hbm, far_ref, near_ref,
    f_buf, mask_buf, cls_buf, rates_ref, sems, rates_sem,
):
    odd = parity("by")
    width = f_hbm.shape[1]
    length = f_hbm.shape[2]
    get_rates = pltpu.make_async_copy(rates_hbm, rates_ref, rates_sem)
    get_rates.start()
    copies = []
    for side in range(2):
        src = pl.ds(side * (length - 1), 1)
        group = [
            pltpu.make_async_copy(f_hbm.at[:, :, src, :], f_buf.at[side], sems.at[side, 0]),
            pltpu.make_async_copy(mask_hbm.at[:, src, :], mask_buf.at[side], sems.at[side, 1]),
            pltpu.make_async_copy(cls_hbm.at[:, src, :], cls_buf.at[side], sems.at[side, 2]),
        ]
        for copy in group:
            copy.start()
        copies.append(group)
    get_rates.wait()
    rates = [rates_ref[k] for k in range(4)]
    leaving = []
    for side in range(2):
        for copy in copies[side]:
            copy.wait()
        f_rows = f_buf.at[side].reshape(19, width, 128)
        mask_rows = mask_buf.at[side].reshape(width, 128)
        cls_rows = cls_buf.at[side].reshape(width, 128)
        for g in range(width // 8):
            fluid = mask_rows[tile(g), :] == 1
            rate = cell_rate(cls_rows[tile(g), :], fluid, rates)
            post, _ = collide([f_rows[q, tile(g), :] for q in range(19)], rate)
            values = [post[q] for q in (UP_Y if side else DOWN_Y)]
            leaving.append(values + [jnp.where(fluid, 1.0, 0.0)])
    for g in range(width // 8):
        for k in range(6):
            low = leaving[g][k]
            high = leaving[width // 8 + g][k]
            far_ref[k, tile(g), :] = jnp.where(odd == 0, low, high)
            near_ref[k, tile(g), :] = jnp.where(odd == 0, high, low)


def first_step(
    f_ref, mask_ref, cls_ref, rates_hbm, order_ref,
    post_ref, flag_ref, rate_ref, edge_ref, edge_flag, edge_rate,
    rates_ref, rates_sem,
):
    del order_ref
    width, length = mask_ref.shape[:2]
    groups = length // 8
    get_rates = pltpu.make_async_copy(rates_hbm, rates_ref, rates_sem)
    get_rates.start()
    get_rates.wait()
    rates = [rates_ref[k] for k in range(4)]

    def plane(x, carry):
        for g in range(groups):
            fluid = mask_ref[x, tile(g), :] == 1
            rate = cell_rate(cls_ref[x, tile(g), :], fluid, rates)
            post, _ = collide([f_ref[q, x, tile(g), :] for q in range(19)], rate)
            for q in range(19):
                post_ref[q, x + 1, tile(g), :] = post[q]
            rate_ref[x, tile(g), :] = rate
            flag = jnp.where(fluid, 1.0, 0.0)
            for step in (-1, 0, 1):
                flag_ref[step + 1, x + 1, tile(g), :] = turn(flag, step)
        return carry

    lax.fori_loop(0, width, plane, 0)
    for e, x in enumerate((0, 1, width - 2, width - 1)):
        for g in range(groups):
            for q in range(19):
                edge_ref[q, e, tile(g), :] = post_ref[q, x + 1, tile(g), :]
            for s in range(3):
                edge_flag[s, e, tile(g), :] = flag_ref[s, x + 1, tile(g), :]
    for s, x in enumerate((0, width - 1)):
        for g in range(groups):
            edge_rate[s, tile(g), :] = rate_ref[x, tile(g), :]


def join_sides(
    post_ref, edge_flag, rate_ref, far_ref, near_ref,
    far_out, near_out, halo_ref, flag_ref, halo_edge, flag_edge, flag_last, row_ref,
):
    odd_x = parity("bx")
    odd_y = parity("by")
    width = far_ref.shape[1]
    length = rate_ref.shape[1]
    groups = length // 8
    for g in range(width // 8):
        for k in range(6):
            far = far_ref[k, tile(g), :]
            near = near_ref[k, tile(g), :]
            low = jnp.where(odd_y == 0, far, near)
            high = jnp.where(odd_y == 0, near, far)
            if k < 5:
                for out_ref in (halo_ref, halo_edge):
                    out_ref[k, tile(g), :] = low
                    out_ref[5 + k, tile(g), :] = high
                continue
            for step in (-1, 0, 1):
                for side, value in enumerate((low, high)):
                    turned = turn(value, step)
                    for out_ref in (flag_ref, flag_edge, flag_last):
                        out_ref[(step + 1) * 2 + side, tile(g), :] = turned

    def outer_plane(s, g):
        own = 0 if s == 0 else 3
        plane_at = 0 if s == 0 else width - 1
        leaving = DOWN_X if s == 0 else UP_X
        arriving = UP_X if s == 0 else DOWN_X
        local = [post_ref[q, own, tile(g), :] for q in range(19)]
        rate = rate_ref[s, tile(g), :]
        fluid = edge_flag[1, own, tile(g), :]

        def load(q, cx, cy, cz):
            def beside():
                return side_row(halo_ref, plane_at - cx, q)

            return shifted(post_ref, q, own - cx, g, cy, beside, beside, step=cz)

        def load_flag(cz, cx, cy):
            return shifted(
                edge_flag, cz + 1, own - cx, g, cy,
                lambda: halo_row(flag_ref, (cz + 1) * 2, plane_at - cx),
                lambda: halo_row(flag_ref, (cz + 1) * 2 + 1, plane_at - cx),
            )

        is_open = open_by_flag(load_flag, fluid)
        f = [local[0]]
        for q in range(1, 19):
            if q in arriving:
                f.append(jnp.zeros_like(fluid))
            else:
                f.append(jnp.where(is_open(q), load(q, *VELOCITY[q]), local[OPPOSITE[q]]))
        return [local[q] for q in leaving] + [fluid] + [f[q] for q in leaving] + list(moments(f)) + [rate]

    for g in range(groups):
        low = outer_plane(0, g)
        high = outer_plane(1, g)
        for k in range(ROWS):
            far_out[k, tile(g), :] = jnp.where(odd_x == 0, low[k], high[k])
            near_out[k, tile(g), :] = jnp.where(odd_x == 0, high[k], low[k])
    for s, x in enumerate((0, width - 1)):
        leaving = DOWN_X if s == 0 else UP_X
        for q in leaving:
            if VELOCITY[q][1] != 0:
                at = 0 if VELOCITY[q][1] == 1 else 1
                row_ref[s, pl.ds(at, 1), :] = side_row(halo_ref, x, q)
        for side in range(2):
            row_ref[s, pl.ds(2 + side, 1), :] = halo_row(flag_ref, 2 + side, x)
    low = row_ref[0]
    high = row_ref[1]
    far_out[ROWS, pl.ds(0, 8), :] = jnp.where(odd_x == 0, low, high)
    near_out[ROWS, pl.ds(0, 8), :] = jnp.where(odd_x == 0, high, low)


def halo_row(ref, k, x):
    return ref[k, pl.ds(x, 1), :]


def second_inner(
    post_ref, flag_ref, rate_ref, halo_ref, halo_flag,
    out_hbm, sums_ref, side_ref, side_copy, own_flag, edge_ref, edge_flag,
    next_ref, out_buf, sems,
):
    width, length = rate_ref.shape[:2]
    groups = length // 8
    chunk = out_buf.shape[2]
    slots = out_buf.shape[0]

    def collide_tile(x, g, carry):
        flux, count = carry
        local = [post_ref[q, x + 1, tile(g), :] for q in range(19)]
        fluid = flag_ref[1, x + 1, tile(g), :]

        def load(q, cx, cy, cz):
            def side():
                return side_row(halo_ref, x - cx, q)

            return shifted(post_ref, q, x + 1 - cx, g, cy, side, side, spare=True, step=cz)

        def load_flag(cz, cx, cy):
            return shifted(
                flag_ref, cz + 1, x + 1 - cx, g, cy,
                lambda: halo_row(halo_flag, (cz + 1) * 2, x - cx),
                lambda: halo_row(halo_flag, (cz + 1) * 2 + 1, x - cx),
                spare=True,
            )

        f, links = pull(local, load, open_by_flag(load_flag, fluid))
        post, mz = collide(f, rate_ref[x, tile(g), :])
        for q in range(19):
            next_ref[q, x, tile(g), :] = post[q]
        flux = flux + link_flux(post, links, mz, fluid)
        count = count + fluid
        return flux, count

    def stream_tile(x, g, slot, j):
        local = [next_ref[q, x, tile(g), :] for q in range(19)]

        def load(q, cx, cy, cz):
            return shifted(next_ref, q, x - cx, g, cy, spare=True, step=cz)

        def load_flag(cz, cx, cy):
            return shifted(flag_ref, cz + 1, x + 1 - cx, g, cy, spare=True)

        f, _ = pull(local, load, open_by_flag(load_flag, flag_ref[1, x + 1, tile(g), :]))
        for q in range(19):
            out_buf[slot, q, j, tile(g), :] = f[q]

    def copy_out(c):
        slot = lax.rem(c, slots)
        return pltpu.make_async_copy(
            out_buf.at[slot], out_hbm.at[:, pl.ds(2 + c * chunk, chunk)], sems.at[slot]
        )

    def first(x, carry):
        for g in range(groups):
            carry = collide_tile(x, g, carry)
        return carry

    zero = jnp.zeros((8, 128), F32)
    carry = lax.fori_loop(1, 4, first, (zero, zero))
    parts = (width - 4) // chunk

    def part(c, carry, steps=chunk):
        slot = lax.rem(c, slots)

        @pl.when(c >= slots)
        def _():
            copy_out(c - slots).wait()

        def step(j, carry):
            x = 2 + c * chunk + j
            for g in range(groups):
                carry = collide_tile(x + 2, g, carry)
                stream_tile(x, g, slot, j)
            return carry

        carry = lax.fori_loop(0, steps, step, carry)
        for j in range(steps, chunk):
            for g in range(groups):
                stream_tile(2 + c * chunk + j, g, slot, j)
        copy_out(c).start()
        return carry

    carry = lax.fori_loop(0, parts - 1, part, carry)
    flux, count = part(parts - 1, carry, chunk - 1)
    sums_ref[0] = flux
    sums_ref[1] = count
    flat = next_ref.reshape(19, width * length, 128)
    flags = flag_ref.reshape(3, (width + 2) * length, 128)
    for g in range(width // 8):
        low_at = pl.ds(g * 8 * length, 8, stride=length)
        high_at = pl.ds(g * 8 * length + length - 1, 8, stride=length)
        for k in range(5):
            low = flat[DOWN_Y[k], low_at, :]
            high = flat[UP_Y[k], high_at, :]
            for to_ref in (side_ref, side_copy):
                to_ref[k, tile(g), :] = low
                to_ref[5 + k, tile(g), :] = high
        own_flag[0, tile(g), :] = flags[1, pl.ds((g * 8 + 1) * length, 8, stride=length), :]
        own_flag[1, tile(g), :] = flags[1, pl.ds((g * 8 + 2) * length - 1, 8, stride=length), :]
    for e, x in enumerate((1, 2, width - 3, width - 2)):
        for g in range(groups):
            for q in range(19):
                edge_ref[q, e, tile(g), :] = next_ref[q, x, tile(g), :]
    for e, x in enumerate((0, 1, 2, width - 3, width - 2, width - 1)):
        for g in range(groups):
            for s in range(3):
                edge_flag[s, e, tile(g), :] = flag_ref[s, x + 1, tile(g), :]
    for c in range(parts - slots, parts):
        copy_out(c).wait()


def second_faces(
    post_ref, flag_ref, rate_ref, halo_ref, halo_flag, sums_ref, side_ref, far_ref, near_ref,
    side_far, side_near, ends_ref, ghost_ref, came_flag, share_ref, came_ref,
):
    odd_x = parity("bx")
    odd_y = parity("by")
    length = rate_ref.shape[1]
    width = side_ref.shape[1]
    groups = length // 8
    flux = sums_ref[0]
    count = sums_ref[1]
    for k in range(ROWS + 1):
        for g in range(groups if k < ROWS else 1):
            far = far_ref[k, tile(g), :]
            near = near_ref[k, tile(g), :]
            came_ref[0, k, tile(g), :] = jnp.where(odd_x == 0, far, near)
            came_ref[1, k, tile(g), :] = jnp.where(odd_x == 0, near, far)
    for s, side in enumerate((1, -1)):
        plane_at = 0 if s == 0 else width - 1
        group = UP_X if side == 1 else DOWN_X
        own = 0 if s == 0 else 3

        for step in (-1, 0, 1):
            for g in range(groups):
                came_flag[step + 1, s, pl.ds(1 + g * 8, 8), :] = turn(came_ref[s, FLAG, tile(g), :], step)
            for end in range(2):
                row = turn(came_ref[s, ROWS, pl.ds(2 + end, 1), :], step)
                came_flag[step + 1, s, pl.ds(end * (length + 1), 1), :] = row
        for g in range(groups):
            local = [post_ref[q, own, tile(g), :] for q in range(19)]
            fluid = flag_ref[1, own, tile(g), :]

            def load(q, cx, cy, cz):
                def beside():
                    return side_row(halo_ref, plane_at - cx, q)

                if cx == side:
                    return shifted(
                        came_ref, s, group.index(q), g, cy,
                        lambda: came_ref[s, ROWS, pl.ds(0, 1), :],
                        lambda: came_ref[s, ROWS, pl.ds(1, 1), :],
                        step=cz,
                    )
                return shifted(post_ref, q, own - cx, g, cy, beside, beside, step=cz)

            def load_flag(cz, cx, cy):
                if cx == side:
                    return came_flag[cz + 1, s, pl.ds(1 + g * 8 - cy, 8), :]
                return shifted(
                    flag_ref, cz + 1, own - cx, g, cy,
                    lambda: halo_row(halo_flag, (cz + 1) * 2, plane_at - cx),
                    lambda: halo_row(halo_flag, (cz + 1) * 2 + 1, plane_at - cx),
                )

            f, links = pull(local, load, open_by_flag(load_flag, fluid))
            post, mz = collide(f, rate_ref[s, tile(g), :])
            for q in range(19):
                ends_ref[q, s, tile(g), :] = post[q]
            flux = flux + link_flux(post, links, mz, fluid)
            count = count + fluid

            beyond_fluid = came_ref[s, FLAG, tile(g), :]
            rho, mx, my, mz = [came_ref[s, SUMS + i, tile(g), :] for i in range(4)]

            def own_flag(cz, cx, cy):
                return shifted(
                    flag_ref, cz + 1, own, g, cy,
                    lambda: halo_row(halo_flag, (cz + 1) * 2, plane_at),
                    lambda: halo_row(halo_flag, (cz + 1) * 2 + 1, plane_at),
                )

            is_open = open_by_flag(own_flag, beyond_fluid)
            for k, toward in enumerate(group):
                q = OPPOSITE[toward]
                _, cy, cz = VELOCITY[q]

                def beside():
                    return side_row(halo_ref, plane_at, q)

                source = shifted(post_ref, q, own, g, cy, beside, beside, step=cz)
                value = jnp.where(is_open(q), source, came_ref[s, k, tile(g), :])
                rho = rho + value
                mx = mx - value if side == 1 else mx + value
                if cy != 0:
                    my = my + value if cy == 1 else my - value
                if cz != 0:
                    mz = mz + value if cz == 1 else mz - value
            f = [None] * 19
            for k, q in enumerate(group):
                f[q] = came_ref[s, NEXT + k, tile(g), :]
            post = relax(f, rho, mx, my, mz, came_ref[s, RATE, tile(g), :])
            for k, q in enumerate(group):
                ghost_ref[k, s, tile(g), :] = post[q]

    for k in range(5):
        for g in range(width // 8):
            low = side_ref[k, tile(g), :]
            high = side_ref[5 + k, tile(g), :]
            side_far[k, tile(g), :] = jnp.where(odd_y == 0, low, high)
            side_near[k, tile(g), :] = jnp.where(odd_y == 0, high, low)
        for s, x in enumerate((0, width - 1)):
            low = ends_ref[DOWN_Y[k], s, pl.ds(0, 1), :]
            high = ends_ref[UP_Y[k], s, pl.ds(length - 1, 1), :]
            side_far[k, pl.ds(x, 1), :] = jnp.where(odd_y == 0, low, high)
            side_near[k, pl.ds(x, 1), :] = jnp.where(odd_y == 0, high, low)
        for s, group, x in ((0, UP_X, width + 1), (1, DOWN_X, width)):
            if DOWN_Y[k] in group:
                low = ghost_ref[group.index(DOWN_Y[k]), s, pl.ds(0, 1), :]
                side_far[k, pl.ds(x, 1), :] = low
                side_near[k, pl.ds(x, 1), :] = low
    for k in range(5):
        for s, group, x in ((0, UP_X, width + 1), (1, DOWN_X, width)):
            if UP_Y[k] in group:
                high = ghost_ref[group.index(UP_Y[k]), s, pl.ds(length - 1, 1), :]
                out_low = side_far[k, pl.ds(x, 1), :]
                side_far[k, pl.ds(x, 1), :] = jnp.where(odd_y == 0, out_low, high)
                side_near[k, pl.ds(x, 1), :] = jnp.where(odd_y == 0, high, out_low)
    lane = lax.broadcasted_iota(jnp.int32, (1, 128), 1)
    total = jnp.sum(jnp.sum(flux, axis=0, keepdims=True), axis=1, keepdims=True)
    cells = jnp.sum(jnp.sum(count, axis=0, keepdims=True), axis=1, keepdims=True)
    row = jnp.where(lane < 64, total, cells)
    share_ref[...] = jnp.broadcast_to(row[None], share_ref.shape)


def mean_flow(share_ref, order_ref, mean_ref):
    del order_ref
    total = jnp.sum(share_ref[:, 0, :], axis=0, keepdims=True)
    lane = lax.broadcasted_iota(jnp.int32, (1, 128), 1)
    flux = jnp.sum(jnp.where(lane == 0, total, 0.0), axis=1, keepdims=True)
    cells = jnp.sum(jnp.where(lane == 127, total, 0.0), axis=1, keepdims=True)
    mean_ref[...] = jnp.broadcast_to(flux / cells, mean_ref.shape)


def last_faces(
    out_in, ends_ref, edge_ref, edge_flag, ghost_ref, came_flag, halo_flag, side_ref, own_flag,
    side_far, side_near,
    out_hbm, halo_ref, out_buf, row_buf, sems, row_sems,
):
    del out_in
    odd_y = parity("by")
    width, length = out_hbm.shape[1:3]
    groups = length // 8
    copies = []
    for k in range(5):
        for g in range(width // 8 + 1):
            far = side_far[k, tile(g), :]
            near = side_near[k, tile(g), :]
            halo_ref[k, tile(g), :] = jnp.where(odd_y == 0, far, near)
            halo_ref[5 + k, tile(g), :] = jnp.where(odd_y == 0, near, far)

    for side, group in enumerate((UP_Y, DOWN_Y)):
        for k, q in enumerate(group):
            cx, _, cz = VELOCITY[q]
            for x in (1, 9, 17, width - 9):
                fluid = own_flag[side, pl.ds(x, 8), :]
                limit = jnp.where(fluid > 0.5, 0.5, 2.0)
                is_open = halo_flag[(cz + 1) * 2 + side, pl.ds(x - cx, 8), :] > limit
                source = turn(halo_ref[side * 5 + k, pl.ds(x - cx, 8), :], cz)
                value = jnp.where(is_open, source, side_ref[side * 5 + k, pl.ds(x, 8), :])
                row_buf[side * 5 + k, pl.ds(x, 8), 0, :] = value
            planes = pl.ds(2, width - 4)
            copy = pltpu.make_async_copy(
                row_buf.at[side * 5 + k, planes],
                out_hbm.at[q, planes, pl.ds(side * (length - 1), 1), :],
                row_sems.at[side * 5 + k],
            )
            copy.start()
            copies.append(copy)

    for s, side in enumerate((1, -1)):
        group = UP_X if side == 1 else DOWN_X
        for outer in (0, 1):
            plane_at = outer if s == 0 else width - 1 - outer
            for g in range(groups):

                def at(plane):
                    if plane == 0:
                        return ends_ref, s
                    return edge_ref, plane - 1 if s == 0 else 4 - plane

                own_ref, own = at(outer)
                local = [own_ref[q, own, tile(g), :] for q in range(19)]

                def load(q, cx, cy, cz):
                    def beside():
                        return side_row(halo_ref, plane_at - cx, q)

                    plane = outer - cx * side
                    if plane < 0:
                        return shifted(ghost_ref, group.index(q), s, g, cy, beside, beside, step=cz)
                    ref, index = at(plane)
                    return shifted(ref, q, index, g, cy, beside, beside, step=cz)

                def load_flag(cz, cx, cy):
                    plane = outer - cx * side
                    if plane < 0:
                        return came_flag[cz + 1, s, pl.ds(1 + g * 8 - cy, 8), :]
                    return shifted(
                        edge_flag, cz + 1, plane if s == 0 else 5 - plane, g, cy,
                        lambda: halo_row(halo_flag, (cz + 1) * 2, plane_at - cx),
                        lambda: halo_row(halo_flag, (cz + 1) * 2 + 1, plane_at - cx),
                    )

                fluid = edge_flag[1, outer if s == 0 else 5 - outer, tile(g), :]
                f, _ = pull(local, load, open_by_flag(load_flag, fluid))
                for q in range(19):
                    out_buf[s, q, outer if s == 0 else 1 - outer, tile(g), :] = f[q]
        planes = pl.ds(0 if s == 0 else width - 2, 2)
        copy = pltpu.make_async_copy(out_buf.at[s], out_hbm.at[:, planes], sems.at[s])
        copy.start()
        copies.append(copy)
    for copy in copies:
        copy.wait()


def whole(count=1):
    return [pl.BlockSpec(memory_space=pltpu.VMEM)] * count


def anywhere(count=1):
    return [pl.BlockSpec(memory_space=pl.ANY)] * count


def vmem(*shape):
    return pltpu.VMEM(shape, F32)


def held(*arrays):
    return [pltpu.with_memory_space_constraint(a, pltpu.VMEM) for a in arrays]


def main_memory(*arrays):
    return [pltpu.with_memory_space_constraint(a, pltpu.HBM) for a in arrays]


def call(kernel, scratch_mib, kib=0, **kwargs):
    return pl.pallas_call(
        kernel,
        cost_estimate=pl.CostEstimate(flops=0, bytes_accessed=kib * 1024, transcendentals=0),
        compiler_params=pltpu.CompilerParams(vmem_limit_bytes=scratch_mib * MIB),
        name=kernel.__name__,
        **kwargs,
    )


def pairs_of(count):
    far = [(i, (i + 1) % count if i % 2 else (i - 1) % count) for i in range(count)]
    near = [(i, i ^ 1) for i in range(count)]
    return far, near


def exchange(far, near, axis):
    far_pairs, near_pairs = pairs_of(lax.axis_size(axis))
    return lax.ppermute(far, axis, far_pairs), lax.ppermute(near, axis, near_pairs)


def body(populations, fluid_mask, rate_class, class_rates):
    width, length, depth = fluid_mask.shape
    count = lax.axis_size("bx") * lax.axis_size("by")
    given = main_memory(populations, fluid_mask, rate_class, class_rates)

    far, near = call(
        first_faces,
        7,
        16384,
        in_specs=anywhere(4),
        out_specs=whole(2),
        out_shape=[vmem(6, width, depth)] * 2,
        scratch_shapes=[
            pltpu.VMEM((2, 19, width, 1, depth), F32),
            pltpu.VMEM((2, width, 1, depth), jnp.int32),
            pltpu.VMEM((2, width, 1, depth), jnp.int32),
            pltpu.SMEM((4,), F32),
            pltpu.SemaphoreType.DMA((2, 3)),
            pltpu.SemaphoreType.DMA,
        ],
    )(*given)
    got_far, got_near = exchange(far, near, "by")

    post, flag, rate, edge, edge_flag, edge_rate = call(
        first_step,
        2,
        in_specs=whole(3) + anywhere(2),
        out_specs=whole(6),
        out_shape=[
            vmem(19, width + 2, length, depth),
            vmem(3, width + 2, length, depth),
            vmem(width, length, depth),
            vmem(19, 4, length, depth),
            vmem(3, 4, length, depth),
            vmem(2, length, depth),
        ],
        scratch_shapes=[pltpu.SMEM((4,), F32), pltpu.SemaphoreType.DMA],
    )(*held(populations, fluid_mask, rate_class), given[3], far)

    far, near, halo, halo_flag, halo_edge, halo_flag_edge, halo_flag_last = call(
        join_sides,
        2,
        in_specs=whole(5),
        out_specs=whole(7),
        out_shape=[vmem(ROWS + 1, length, depth)] * 2
        + [vmem(10, width, depth), vmem(6, width, depth)] * 2
        + [vmem(6, width, depth)],
        scratch_shapes=[pltpu.VMEM((2, 8, depth), F32)],
    )(*held(edge, edge_flag, edge_rate, got_far, got_near))
    got_far, got_near = exchange(far, near, "bx")

    final, sums, side, side_copy, own_flag, after_edge, last_flag = call(
        second_inner,
        16,
        in_specs=whole(5),
        out_specs=anywhere(1) + whole(6),
        out_shape=[
            pltpu.HBM(populations.shape, F32),
            vmem(2, 8, depth),
            vmem(10, width, depth),
            vmem(10, width, depth),
            vmem(2, width, depth),
            vmem(19, 4, length, depth),
            vmem(3, 6, length, depth),
        ],
        scratch_shapes=[
            pltpu.VMEM((19, width, length, depth), F32),
            pltpu.VMEM((3, 19, 4, length, depth), F32),
            pltpu.SemaphoreType.DMA((3,)),
        ],
    )(*held(post, flag, rate, halo, halo_flag))

    side_far, side_near, ends, ghost, came_flag, share = call(
        second_faces,
        3,
        in_specs=whole(9),
        out_specs=whole(6),
        out_shape=[vmem(5, width + 8, depth)] * 2
        + [
            vmem(19, 2, length, depth),
            vmem(5, 2, length, depth),
            vmem(3, 2, length + 8, depth),
            vmem(count, 2, depth),
        ],
        scratch_shapes=[pltpu.VMEM((2, ROWS + 1, length, depth), F32)],
    )(*held(edge, edge_flag, edge_rate, halo_edge, halo_flag_edge, sums, side, got_far, got_near))
    side_far, side_near = exchange(side_far, side_near, "by")
    share = lax.all_to_all(share, ("bx", "by"), 0, 0)

    final = call(
        last_faces,
        6,
        in_specs=anywhere(1) + whole(10),
        out_specs=anywhere(1)[0],
        out_shape=pltpu.HBM(populations.shape, F32),
        scratch_shapes=[
            pltpu.VMEM((10, width + 8, depth), F32),
            pltpu.VMEM((2, 19, 2, length, depth), F32),
            pltpu.VMEM((10, width, 1, depth), F32),
            pltpu.SemaphoreType.DMA((2,)),
            pltpu.SemaphoreType.DMA((10,)),
        ],
        input_output_aliases={0: 0},
    )(
        *main_memory(final),
        *held(ends, after_edge, last_flag, ghost, came_flag, halo_flag_last, side_copy, own_flag),
        *held(side_far, side_near),
    )
    mean = call(
        mean_flow,
        2,
        in_specs=whole(1) + anywhere(1),
        out_specs=whole(1)[0],
        out_shape=jax.ShapeDtypeStruct((1, depth), F32),
    )(*held(share), *main_memory(final))
    return final, mean[0, :1]


def solution(mesh):
    placed = (P(None, "bx", "by", None), P("bx", "by", None), P("bx", "by", None), P())
    return jax.shard_map(
        body,
        mesh=mesh,
        in_specs=placed,
        out_specs=(P(None, "bx", "by", None), P()),
        check_vma=False,
    )
```

```python
import jax
import jax.numpy as jnp
from jax import lax
from jax.experimental import pallas as pl
from jax.experimental.pallas import tpu as pltpu
from jax.sharding import PartitionSpec as P

VELOCITY = [
    (0, 0, 0),
    (1, 0, 0),
    (-1, 0, 0),
    (0, 1, 0),
    (0, -1, 0),
    (0, 0, 1),
    (0, 0, -1),
    (1, 1, 0),
    (-1, -1, 0),
    (1, -1, 0),
    (-1, 1, 0),
    (1, 0, 1),
    (-1, 0, -1),
    (1, 0, -1),
    (-1, 0, 1),
    (0, 1, 1),
    (0, -1, -1),
    (0, 1, -1),
    (0, -1, 1),
]
OPPOSITE = [0, 2, 1, 4, 3, 6, 5, 8, 7, 10, 9, 12, 11, 14, 13, 16, 15, 18, 17]
UP_X = [q for q in range(19) if VELOCITY[q][0] == 1]
DOWN_X = [OPPOSITE[q] for q in UP_X]
UP_Y = [q for q in range(19) if VELOCITY[q][1] == 1]
DOWN_Y = [OPPOSITE[q] for q in UP_Y]
FLAG, NEXT, SUMS, RATE, ROWS = 5, 6, 11, 15, 16
F32 = jnp.float32
MIB = 1024 * 1024


def collide(f, rate):
    rho, mx, my, mz = moments(f)
    return relax(f, rho, mx, my, mz, rate), mz


def moments(f):
    plus = {}
    diff = {}
    for q in range(1, 19, 2):
        plus[q] = f[q] + f[q + 1]
        diff[q] = f[q] - f[q + 1]
    rho = ((f[0] + plus[1]) + (plus[3] + plus[5])) + (
        ((plus[7] + plus[9]) + (plus[11] + plus[13])) + (plus[15] + plus[17])
    )
    mx = (diff[1] + diff[7]) + (diff[9] + diff[11]) + diff[13]
    my = (diff[3] + diff[7]) + (diff[15] - diff[9]) + diff[17]
    mz = (diff[5] + diff[11]) + (diff[15] - diff[13]) - diff[17]
    return rho, mx, my, mz


def relax(f, rho, mx, my, mz, rate):
    inv = 4.5 / rho
    ux = inv * mx
    uy = inv * my
    uz = inv * mz
    tx = ux * mx
    ty = uy * my
    tz = uz * mz
    base = rho - ((tx + ty) + tz) * (1.0 / 3.0)
    keep = 1.0 - rate
    r36 = rate * (1.0 / 36.0)
    r18 = rate * (1.0 / 18.0)
    r12 = rate * (1.0 / 12.0)
    gx = r12 * mx
    gy = r12 * my
    gz = r12 * mz
    ux2 = ux + ux
    uy2 = uy + uy
    cross = {7: ux2 * my, 11: ux2 * mz, 15: uy2 * mz}
    pair_base = {7: base + (tx + ty), 11: base + (tx + tz), 15: base + (ty + tz)}
    lean = {7: (gx, gy), 11: (gx, gz), 15: (gy, gz)}
    out = [None] * 19

    def put(q, even, odd):
        if f[q] is not None:
            out[q] = keep * f[q] + (even + odd)
        if f[q + 1] is not None:
            out[q + 1] = keep * f[q + 1] + (even - odd)

    if f[0] is not None:
        out[0] = keep * f[0] + (rate * (1.0 / 3.0)) * base
    for q, t, g in ((1, tx, gx), (3, ty, gy), (5, tz, gz)):
        put(q, r18 * (base + t), g + g)
    for q in (7, 11, 15):
        one, two = lean[q]
        put(q, r36 * (pair_base[q] + cross[q]), one + two)
        put(q + 2, r36 * (pair_base[q] - cross[q]), one - two)
    return out


def turn(value, step):
    if step == 0:
        return value
    return pltpu.roll(value, step % value.shape[-1], axis=value.ndim - 1)


def cell_rate(cls, fluid, rates):
    rate = jnp.where(cls == 0, rates[0], rates[1])
    rate = jnp.where(cls == 2, rates[2], rate)
    rate = jnp.where(cls == 3, rates[3], rate)
    return jnp.where(fluid, rate, 0.0)


def pull(local, load, is_open):
    out = [local[0]]
    links = [None]
    for q in range(1, 19):
        links.append(is_open(q))
        out.append(jnp.where(links[q], load(q, *VELOCITY[q]), local[OPPOSITE[q]]))
    return out, links


def open_by_flag(load_flag, fluid):
    limit = jnp.where(fluid > 0.5, 0.5, 2.0)

    def is_open(q):
        move = VELOCITY[q]
        return load_flag(move[2], move[0], move[1]) > limit

    return is_open


def link_flux(post, links, mz, fluid):
    total = None
    for q in range(19):
        step = VELOCITY[q][2]
        if step == 0:
            continue
        term = jnp.where(links[OPPOSITE[q]], post[q], 0.0)
        if total is None:
            total = term if step > 0 else -term
        else:
            total = total + term if step > 0 else total - term
    return (total + total) - jnp.where(fluid > 0.5, mz, 0.0)


def beyond(ref, k, plane, g, cy, spare):
    length = ref.shape[2]
    if not spare:
        return pltpu.roll(ref[k, plane, tile(g), :], cy % 8, axis=0)
    flat = ref.reshape(ref.shape[0], ref.shape[1] * length, ref.shape[3])
    return flat[k, pl.ds(plane * length + (g * 8 - cy), 8), :]


def shifted(ref, k, plane, g, cy, low=None, high=None, spare=False, step=0):
    groups = ref.shape[2] // 8
    if cy == 1 and g == 0:
        value = beyond(ref, k, plane, g, cy, spare)
        if low is not None:
            value = jnp.where(lax.broadcasted_iota(jnp.int32, value.shape, 0) == 0, low(), value)
        return turn(value, step)
    if cy == -1 and g == groups - 1:
        value = beyond(ref, k, plane, g, cy, spare)
        if high is not None:
            value = jnp.where(lax.broadcasted_iota(jnp.int32, value.shape, 0) == 7, high(), value)
        return turn(value, step)
    return turn(ref[k, plane, pl.ds(g * 8 - cy, 8), :], step)


def side_row(halo_ref, x, q):
    if isinstance(x, int) and x < 0:
        x = 33
    k = UP_Y.index(q) if q in UP_Y else 5 + DOWN_Y.index(q)
    return halo_ref[k, pl.ds(x, 1), :]


def tile(g):
    return pl.ds(g * 8, 8)


def parity(axis):
    return lax.rem(lax.axis_index(axis), 2)


def first_faces(
    f_hbm, mask_hbm, cls_hbm, rates_hbm, near_ref, far_ref, rates_out,
    f_buf, mask_buf, cls_buf, rates_ref, sems, rates_sem,
):
    odd = parity("by")
    width = f_hbm.shape[1]
    length = f_hbm.shape[2]
    get_rates = pltpu.make_async_copy(rates_hbm, rates_ref, rates_sem)
    get_rates.start()
    copies = []
    for side in range(2):
        src = pl.ds(side * (length - 1), 1)
        group = [
            pltpu.make_async_copy(f_hbm.at[:, :, src, :], f_buf.at[side], sems.at[side, 0]),
            pltpu.make_async_copy(mask_hbm.at[:, src, :], mask_buf.at[side], sems.at[side, 1]),
            pltpu.make_async_copy(cls_hbm.at[:, src, :], cls_buf.at[side], sems.at[side, 2]),
        ]
        for copy in group:
            copy.start()
        copies.append(group)
    get_rates.wait()
    rates = [rates_ref[k] for k in range(4)]
    for k in range(4):
        rates_out[pl.ds(k, 1), :] = jnp.full((1, 128), rates[k], F32)
    leaving = []
    for side in range(2):
        for copy in copies[side]:
            copy.wait()
        f_rows = f_buf.at[side].reshape(19, width, 128)
        mask_rows = mask_buf.at[side].reshape(width, 128)
        cls_rows = cls_buf.at[side].reshape(width, 128)
        for g in range(width // 8):
            fluid = mask_rows[tile(g), :] == 1
            rate = cell_rate(cls_rows[tile(g), :], fluid, rates)
            post, _ = collide([f_rows[q, tile(g), :] for q in range(19)], rate)
            values = [post[q] for q in (UP_Y if side else DOWN_Y)]
            leaving.append(values + [jnp.where(fluid, 1.0, 0.0)])
    for g in range(width // 8):
        for k in range(6):
            low = leaving[g][k]
            high = leaving[width // 8 + g][k]
            far_ref[k, tile(g), :] = jnp.where(odd == 0, low, high)
            near_ref[k, tile(g), :] = jnp.where(odd == 0, high, low)


def first_step(
    f_ref, mask_ref, cls_ref, rates_ref,
    post_ref, flag_ref, rate_ref, edge_ref, edge_flag, edge_rate,
):
    width, length = mask_ref.shape[:2]
    groups = length // 8
    rates = [jnp.broadcast_to(rates_ref[pl.ds(k, 1), :], (8, 128)) for k in range(4)]

    def plane(x, carry):
        for g in range(groups):
            fluid = mask_ref[x, tile(g), :] == 1
            rate = cell_rate(cls_ref[x, tile(g), :], fluid, rates)
            post, _ = collide([f_ref[q, x, tile(g), :] for q in range(19)], rate)
            for q in range(19):
                post_ref[q, x + 1, tile(g), :] = post[q]
            rate_ref[x, tile(g), :] = rate
            flag = jnp.where(fluid, 1.0, 0.0)
            for step in (-1, 0, 1):
                flag_ref[step + 1, x + 1, tile(g), :] = turn(flag, step)
        return carry

    lax.fori_loop(0, width, plane, 0, unroll=2)
    for e, x in enumerate((0, 1, width - 2, width - 1)):
        for g in range(groups):
            for q in range(19):
                edge_ref[q, e, tile(g), :] = post_ref[q, x + 1, tile(g), :]
            for s in range(3):
                edge_flag[s, e, tile(g), :] = flag_ref[s, x + 1, tile(g), :]
    for s, x in enumerate((0, width - 1)):
        for g in range(groups):
            edge_rate[s, tile(g), :] = rate_ref[x, tile(g), :]


def join_sides(
    post_ref, edge_flag, rate_ref, near_ref, far_ref,
    far_out, near_out, halo_ref, flag_ref, halo_edge, flag_edge, flag_last, row_ref,
):
    odd_x = parity("bx")
    odd_y = parity("by")
    width = far_ref.shape[1]
    length = rate_ref.shape[1]
    groups = length // 8
    for g in range(width // 8):
        for k in range(6):
            far = far_ref[k, tile(g), :]
            near = near_ref[k, tile(g), :]
            low = jnp.where(odd_y == 0, far, near)
            high = jnp.where(odd_y == 0, near, far)
            if k < 5:
                for out_ref in (halo_ref, halo_edge):
                    out_ref[k, tile(g), :] = low
                    out_ref[5 + k, tile(g), :] = high
                continue
            for step in (-1, 0, 1):
                for side, value in enumerate((low, high)):
                    turned = turn(value, step)
                    for out_ref in (flag_ref, flag_edge, flag_last):
                        out_ref[(step + 1) * 2 + side, tile(g), :] = turned

    def outer_plane(s, g):
        own = 0 if s == 0 else 3
        plane_at = 0 if s == 0 else width - 1
        leaving = DOWN_X if s == 0 else UP_X
        arriving = UP_X if s == 0 else DOWN_X
        local = [post_ref[q, own, tile(g), :] for q in range(19)]
        rate = rate_ref[s, tile(g), :]
        fluid = edge_flag[1, own, tile(g), :]

        def load(q, cx, cy, cz):
            def beside():
                return side_row(halo_ref, plane_at - cx, q)

            return shifted(post_ref, q, own - cx, g, cy, beside, beside, step=cz)

        def load_flag(cz, cx, cy):
            return shifted(
                edge_flag, cz + 1, own - cx, g, cy,
                lambda: halo_row(flag_ref, (cz + 1) * 2, plane_at - cx),
                lambda: halo_row(flag_ref, (cz + 1) * 2 + 1, plane_at - cx),
            )

        is_open = open_by_flag(load_flag, fluid)
        f = [local[0]]
        for q in range(1, 19):
            if q in arriving:
                f.append(jnp.zeros_like(fluid))
            else:
                f.append(jnp.where(is_open(q), load(q, *VELOCITY[q]), local[OPPOSITE[q]]))
        return [local[q] for q in leaving] + [fluid] + [f[q] for q in leaving] + list(moments(f)) + [rate]

    for g in range(groups):
        low = outer_plane(0, g)
        high = outer_plane(1, g)
        for k in range(ROWS):
            far_out[k, tile(g), :] = jnp.where(odd_x == 0, low[k], high[k])
            near_out[k, tile(g), :] = jnp.where(odd_x == 0, high[k], low[k])
    for s, x in enumerate((0, width - 1)):
        leaving = DOWN_X if s == 0 else UP_X
        for q in leaving:
            if VELOCITY[q][1] != 0:
                at = 0 if VELOCITY[q][1] == 1 else 1
                row_ref[s, pl.ds(at, 1), :] = side_row(halo_ref, x, q)
        for side in range(2):
            row_ref[s, pl.ds(2 + side, 1), :] = halo_row(flag_ref, 2 + side, x)
    low = row_ref[0]
    high = row_ref[1]
    far_out[ROWS, pl.ds(0, 8), :] = jnp.where(odd_x == 0, low, high)
    near_out[ROWS, pl.ds(0, 8), :] = jnp.where(odd_x == 0, high, low)


def halo_row(ref, k, x):
    return ref[k, pl.ds(x, 1), :]


def second_inner(
    post_ref, flag_ref, rate_ref, halo_ref, halo_flag,
    out_hbm, sums_ref, side_ref, side_copy, own_flag, edge_ref, edge_flag,
    next_ref, out_buf, sems, last_sems,
):
    width, length = rate_ref.shape[:2]
    groups = length // 8
    chunk = out_buf.shape[2]
    slots = out_buf.shape[0]

    def collide_tile(x, g, carry):
        flux, count = carry
        local = [post_ref[q, x + 1, tile(g), :] for q in range(19)]
        fluid = flag_ref[1, x + 1, tile(g), :]

        def load(q, cx, cy, cz):
            def side():
                return side_row(halo_ref, x - cx, q)

            return shifted(post_ref, q, x + 1 - cx, g, cy, side, side, spare=True, step=cz)

        def load_flag(cz, cx, cy):
            return shifted(
                flag_ref, cz + 1, x + 1 - cx, g, cy,
                lambda: halo_row(halo_flag, (cz + 1) * 2, x - cx),
                lambda: halo_row(halo_flag, (cz + 1) * 2 + 1, x - cx),
                spare=True,
            )

        f, links = pull(local, load, open_by_flag(load_flag, fluid))
        post, mz = collide(f, rate_ref[x, tile(g), :])
        for q in range(19):
            next_ref[q, x, tile(g), :] = post[q]
        flux = flux + link_flux(post, links, mz, fluid)
        count = count + fluid
        return flux, count

    def stream_tile(x, g, slot, j):
        local = [next_ref[q, x, tile(g), :] for q in range(19)]

        def load(q, cx, cy, cz):
            return shifted(next_ref, q, x - cx, g, cy, spare=True, step=cz)

        def load_flag(cz, cx, cy):
            return shifted(flag_ref, cz + 1, x + 1 - cx, g, cy, spare=True)

        f, _ = pull(local, load, open_by_flag(load_flag, flag_ref[1, x + 1, tile(g), :]))
        for q in range(19):
            out_buf[slot, q, j, tile(g), :] = f[q]

    def copy_out(c):
        slot = lax.rem(c, slots)
        return pltpu.make_async_copy(
            out_buf.at[slot], out_hbm.at[:, pl.ds(2 + c * chunk, chunk)], sems.at[slot]
        )

    def first(x, carry):
        for g in range(groups):
            carry = collide_tile(x, g, carry)
        return carry

    zero = jnp.zeros((8, 128), F32)
    carry = lax.fori_loop(1, 4, first, (zero, zero))
    parts = (width - 4) // chunk

    def part(c, carry, steps=chunk):
        slot = lax.rem(c, slots)

        @pl.when(c >= slots)
        def _():
            copy_out(c - slots).wait()

        def step(j, carry):
            x = 2 + c * chunk + j
            for g in range(groups):
                stream_tile(x, g, slot, j)
            for g in range(groups):
                carry = collide_tile(x + 2, g, carry)
            return carry

        carry = lax.fori_loop(0, steps, step, carry, unroll=steps if steps == chunk else 1)
        if steps == chunk:
            copy_out(c).start()
        return carry

    carry = lax.fori_loop(0, parts - 1, part, carry)
    last_slot = (parts - 1) % slots
    last_x = 2 + (parts - 1) * chunk

    def copy_last(j, planes):
        return pltpu.make_async_copy(
            out_buf.at[last_slot, :, pl.ds(j, planes)],
            out_hbm.at[:, pl.ds(last_x + j, planes)],
            last_sems.at[j],
        )

    flux, count = part(parts - 1, carry, chunk - 1)
    copy_last(0, chunk - 1).start()
    for g in range(groups):
        stream_tile(last_x + chunk - 1, g, last_slot, chunk - 1)
    copy_last(chunk - 1, 1).start()
    sums_ref[0] = flux
    sums_ref[1] = count
    flat = next_ref.reshape(19, width * length, 128)
    flags = flag_ref.reshape(3, (width + 2) * length, 128)
    for g in range(width // 8):
        low_at = pl.ds(g * 8 * length, 8, stride=length)
        high_at = pl.ds(g * 8 * length + length - 1, 8, stride=length)
        for k in range(5):
            low = flat[DOWN_Y[k], low_at, :]
            high = flat[UP_Y[k], high_at, :]
            for to_ref in (side_ref, side_copy):
                to_ref[k, tile(g), :] = low
                to_ref[5 + k, tile(g), :] = high
        own_flag[0, tile(g), :] = flags[1, pl.ds((g * 8 + 1) * length, 8, stride=length), :]
        own_flag[1, tile(g), :] = flags[1, pl.ds((g * 8 + 2) * length - 1, 8, stride=length), :]
    for e, x in enumerate((1, 2, width - 3, width - 2)):
        for g in range(groups):
            for q in range(19):
                edge_ref[q, e, tile(g), :] = next_ref[q, x, tile(g), :]
    for e, x in enumerate((0, 1, 2, width - 3, width - 2, width - 1)):
        for g in range(groups):
            for s in range(3):
                edge_flag[s, e, tile(g), :] = flag_ref[s, x + 1, tile(g), :]
    for c in range(parts - slots, parts - 1):
        copy_out(c).wait()
    copy_last(0, chunk - 1).wait()
    copy_last(chunk - 1, 1).wait()


def second_faces(
    post_ref, flag_ref, rate_ref, halo_ref, halo_flag, sums_ref, side_ref, far_ref, near_ref,
    side_near, side_far, ends_ref, ghost_ref, came_flag, share_ref, came_ref,
):
    odd_x = parity("bx")
    odd_y = parity("by")
    length = rate_ref.shape[1]
    width = side_ref.shape[1]
    groups = length // 8
    flux = sums_ref[0]
    count = sums_ref[1]
    for k in range(ROWS + 1):
        for g in range(groups if k < ROWS else 1):
            far = far_ref[k, tile(g), :]
            near = near_ref[k, tile(g), :]
            came_ref[0, k, tile(g), :] = jnp.where(odd_x == 0, far, near)
            came_ref[1, k, tile(g), :] = jnp.where(odd_x == 0, near, far)
    for s, side in enumerate((1, -1)):
        plane_at = 0 if s == 0 else width - 1
        group = UP_X if side == 1 else DOWN_X
        own = 0 if s == 0 else 3

        for step in (-1, 0, 1):
            for g in range(groups):
                came_flag[step + 1, s, pl.ds(1 + g * 8, 8), :] = turn(came_ref[s, FLAG, tile(g), :], step)
            for end in range(2):
                row = turn(came_ref[s, ROWS, pl.ds(2 + end, 1), :], step)
                came_flag[step + 1, s, pl.ds(end * (length + 1), 1), :] = row
        for g in range(groups):
            local = [post_ref[q, own, tile(g), :] for q in range(19)]
            fluid = flag_ref[1, own, tile(g), :]

            def load(q, cx, cy, cz):
                def beside():
                    return side_row(halo_ref, plane_at - cx, q)

                if cx == side:
                    return shifted(
                        came_ref, s, group.index(q), g, cy,
                        lambda: came_ref[s, ROWS, pl.ds(0, 1), :],
                        lambda: came_ref[s, ROWS, pl.ds(1, 1), :],
                        step=cz,
                    )
                return shifted(post_ref, q, own - cx, g, cy, beside, beside, step=cz)

            def load_flag(cz, cx, cy):
                if cx == side:
                    return came_flag[cz + 1, s, pl.ds(1 + g * 8 - cy, 8), :]
                return shifted(
                    flag_ref, cz + 1, own - cx, g, cy,
                    lambda: halo_row(halo_flag, (cz + 1) * 2, plane_at - cx),
                    lambda: halo_row(halo_flag, (cz + 1) * 2 + 1, plane_at - cx),
                )

            f, links = pull(local, load, open_by_flag(load_flag, fluid))
            post, mz = collide(f, rate_ref[s, tile(g), :])
            for q in range(19):
                ends_ref[q, s, tile(g), :] = post[q]
            flux = flux + link_flux(post, links, mz, fluid)
            count = count + fluid

            beyond_fluid = came_ref[s, FLAG, tile(g), :]
            rho, mx, my, mz = [came_ref[s, SUMS + i, tile(g), :] for i in range(4)]

            def own_flag(cz, cx, cy):
                return shifted(
                    flag_ref, cz + 1, own, g, cy,
                    lambda: halo_row(halo_flag, (cz + 1) * 2, plane_at),
                    lambda: halo_row(halo_flag, (cz + 1) * 2 + 1, plane_at),
                )

            is_open = open_by_flag(own_flag, beyond_fluid)
            for k, toward in enumerate(group):
                q = OPPOSITE[toward]
                _, cy, cz = VELOCITY[q]

                def beside():
                    return side_row(halo_ref, plane_at, q)

                source = shifted(post_ref, q, own, g, cy, beside, beside, step=cz)
                value = jnp.where(is_open(q), source, came_ref[s, k, tile(g), :])
                rho = rho + value
                mx = mx - value if side == 1 else mx + value
                if cy != 0:
                    my = my + value if cy == 1 else my - value
                if cz != 0:
                    mz = mz + value if cz == 1 else mz - value
            f = [None] * 19
            for k, q in enumerate(group):
                f[q] = came_ref[s, NEXT + k, tile(g), :]
            post = relax(f, rho, mx, my, mz, came_ref[s, RATE, tile(g), :])
            for k, q in enumerate(group):
                ghost_ref[k, s, tile(g), :] = post[q]

    for k in range(5):
        for g in range(width // 8):
            low = side_ref[k, tile(g), :]
            high = side_ref[5 + k, tile(g), :]
            side_far[k, tile(g), :] = jnp.where(odd_y == 0, low, high)
            side_near[k, tile(g), :] = jnp.where(odd_y == 0, high, low)
        for s, x in enumerate((0, width - 1)):
            low = ends_ref[DOWN_Y[k], s, pl.ds(0, 1), :]
            high = ends_ref[UP_Y[k], s, pl.ds(length - 1, 1), :]
            side_far[k, pl.ds(x, 1), :] = jnp.where(odd_y == 0, low, high)
            side_near[k, pl.ds(x, 1), :] = jnp.where(odd_y == 0, high, low)
        for s, group, x in ((0, UP_X, width + 1), (1, DOWN_X, width)):
            if DOWN_Y[k] in group:
                low = ghost_ref[group.index(DOWN_Y[k]), s, pl.ds(0, 1), :]
                side_far[k, pl.ds(x, 1), :] = low
                side_near[k, pl.ds(x, 1), :] = low
    for k in range(5):
        for s, group, x in ((0, UP_X, width + 1), (1, DOWN_X, width)):
            if UP_Y[k] in group:
                high = ghost_ref[group.index(UP_Y[k]), s, pl.ds(length - 1, 1), :]
                out_low = side_far[k, pl.ds(x, 1), :]
                side_far[k, pl.ds(x, 1), :] = jnp.where(odd_y == 0, out_low, high)
                side_near[k, pl.ds(x, 1), :] = jnp.where(odd_y == 0, high, out_low)
    lane = lax.broadcasted_iota(jnp.int32, (1, 128), 1)
    total = jnp.sum(jnp.sum(flux, axis=0, keepdims=True), axis=1, keepdims=True)
    cells = jnp.sum(jnp.sum(count, axis=0, keepdims=True), axis=1, keepdims=True)
    row = jnp.where(lane < 64, total, cells)
    share_ref[...] = jnp.broadcast_to(row[None], share_ref.shape)


def mean_flow(share_ref, order_ref, mean_ref):
    del order_ref
    total = jnp.sum(share_ref[:, 0, :], axis=0, keepdims=True)
    lane = lax.broadcasted_iota(jnp.int32, (1, 128), 1)
    flux = jnp.sum(jnp.where(lane == 0, total, 0.0), axis=1, keepdims=True)
    cells = jnp.sum(jnp.where(lane == 127, total, 0.0), axis=1, keepdims=True)
    mean_ref[...] = jnp.broadcast_to(flux / cells, mean_ref.shape)


def last_faces(
    out_in, ends_ref, edge_ref, edge_flag, ghost_ref, came_flag, halo_flag, side_ref, own_flag,
    side_near, side_far,
    out_hbm, halo_ref, out_buf, row_buf, sems, row_sems,
):
    del out_in
    odd_y = parity("by")
    width, length = out_hbm.shape[1:3]
    groups = length // 8
    copies = []
    for k in range(5):
        for g in range(width // 8 + 1):
            far = side_far[k, tile(g), :]
            near = side_near[k, tile(g), :]
            halo_ref[k, tile(g), :] = jnp.where(odd_y == 0, far, near)
            halo_ref[5 + k, tile(g), :] = jnp.where(odd_y == 0, near, far)

    for side, group in enumerate((UP_Y, DOWN_Y)):
        for k, q in enumerate(group):
            cx, _, cz = VELOCITY[q]
            for x in (1, 9, 17, width - 9):
                fluid = own_flag[side, pl.ds(x, 8), :]
                limit = jnp.where(fluid > 0.5, 0.5, 2.0)
                is_open = halo_flag[(cz + 1) * 2 + side, pl.ds(x - cx, 8), :] > limit
                source = turn(halo_ref[side * 5 + k, pl.ds(x - cx, 8), :], cz)
                value = jnp.where(is_open, source, side_ref[side * 5 + k, pl.ds(x, 8), :])
                row_buf[side * 5 + k, pl.ds(x, 8), 0, :] = value
            planes = pl.ds(2, width - 4)
            copy = pltpu.make_async_copy(
                row_buf.at[side * 5 + k, planes],
                out_hbm.at[q, planes, pl.ds(side * (length - 1), 1), :],
                row_sems.at[side * 5 + k],
            )
            copy.start()
            copies.append(copy)

    for s, side in enumerate((1, -1)):
        group = UP_X if side == 1 else DOWN_X
        for outer in (0, 1):
            plane_at = outer if s == 0 else width - 1 - outer
            for g in range(groups):

                def at(plane):
                    if plane == 0:
                        return ends_ref, s
                    return edge_ref, plane - 1 if s == 0 else 4 - plane

                own_ref, own = at(outer)
                local = [own_ref[q, own, tile(g), :] for q in range(19)]

                def load(q, cx, cy, cz):
                    def beside():
                        return side_row(halo_ref, plane_at - cx, q)

                    plane = outer - cx * side
                    if plane < 0:
                        return shifted(ghost_ref, group.index(q), s, g, cy, beside, beside, step=cz)
                    ref, index = at(plane)
                    return shifted(ref, q, index, g, cy, beside, beside, step=cz)

                def load_flag(cz, cx, cy):
                    plane = outer - cx * side
                    if plane < 0:
                        return came_flag[cz + 1, s, pl.ds(1 + g * 8 - cy, 8), :]
                    return shifted(
                        edge_flag, cz + 1, plane if s == 0 else 5 - plane, g, cy,
                        lambda: halo_row(halo_flag, (cz + 1) * 2, plane_at - cx),
                        lambda: halo_row(halo_flag, (cz + 1) * 2 + 1, plane_at - cx),
                    )

                fluid = edge_flag[1, outer if s == 0 else 5 - outer, tile(g), :]
                f, _ = pull(local, load, open_by_flag(load_flag, fluid))
                for q in range(19):
                    out_buf[s, q, outer if s == 0 else 1 - outer, tile(g), :] = f[q]
        planes = pl.ds(0 if s == 0 else width - 2, 2)
        copy = pltpu.make_async_copy(out_buf.at[s], out_hbm.at[:, planes], sems.at[s])
        copy.start()
        copies.append(copy)
    for copy in copies:
        copy.wait()


def whole(count=1):
    return [pl.BlockSpec(memory_space=pltpu.VMEM)] * count


def anywhere(count=1):
    return [pl.BlockSpec(memory_space=pl.ANY)] * count


def vmem(*shape):
    return pltpu.VMEM(shape, F32)


def held(*arrays):
    return [pltpu.with_memory_space_constraint(a, pltpu.VMEM) for a in arrays]


def main_memory(*arrays):
    return [pltpu.with_memory_space_constraint(a, pltpu.HBM) for a in arrays]


def call(kernel, scratch_mib, kib=0, **kwargs):
    return pl.pallas_call(
        kernel,
        cost_estimate=pl.CostEstimate(flops=0, bytes_accessed=kib * 1024, transcendentals=0),
        compiler_params=pltpu.CompilerParams(vmem_limit_bytes=scratch_mib * MIB),
        name=kernel.__name__,
        **kwargs,
    )


def pairs_of(count):
    far = [(i, (i + 1) % count if i % 2 else (i - 1) % count) for i in range(count)]
    near = [(i, i ^ 1) for i in range(count)]
    return far, near


def exchange(far, near, axis):
    far_pairs, near_pairs = pairs_of(lax.axis_size(axis))
    return lax.ppermute(far, axis, far_pairs), lax.ppermute(near, axis, near_pairs)


def body(populations, fluid_mask, rate_class, class_rates):
    width, length, depth = fluid_mask.shape
    count = lax.axis_size("bx") * lax.axis_size("by")
    given = main_memory(populations, fluid_mask, rate_class, class_rates)

    near, far, rates = call(
        first_faces,
        7,
        16384,
        in_specs=anywhere(4),
        out_specs=whole(3),
        out_shape=[vmem(6, width, depth)] * 2 + [vmem(8, depth)],
        scratch_shapes=[
            pltpu.VMEM((2, 19, width, 1, depth), F32),
            pltpu.VMEM((2, width, 1, depth), jnp.int32),
            pltpu.VMEM((2, width, 1, depth), jnp.int32),
            pltpu.SMEM((4,), F32),
            pltpu.SemaphoreType.DMA((2, 3)),
            pltpu.SemaphoreType.DMA,
        ],
    )(*given)
    got_far, got_near = exchange(far, near, "by")

    post, flag, rate, edge, edge_flag, edge_rate = call(
        first_step,
        2,
        in_specs=whole(4),
        out_specs=whole(6),
        out_shape=[
            vmem(19, width + 2, length, depth),
            vmem(3, width + 2, length, depth),
            vmem(width, length, depth),
            vmem(19, 4, length, depth),
            vmem(3, 4, length, depth),
            vmem(2, length, depth),
        ],
    )(*held(populations, fluid_mask, rate_class, rates))

    far, near, halo, halo_flag, halo_edge, halo_flag_edge, halo_flag_last = call(
        join_sides,
        2,
        in_specs=whole(5),
        out_specs=whole(7),
        out_shape=[vmem(ROWS + 1, length, depth)] * 2
        + [vmem(10, width, depth), vmem(6, width, depth)] * 2
        + [vmem(6, width, depth)],
        scratch_shapes=[pltpu.VMEM((2, 8, depth), F32)],
    )(*held(edge, edge_flag, edge_rate, got_near, got_far))
    got_far, got_near = exchange(far, near, "bx")

    final, sums, side, side_copy, own_flag, after_edge, last_flag = call(
        second_inner,
        16,
        in_specs=whole(5),
        out_specs=anywhere(1) + whole(6),
        out_shape=[
            pltpu.HBM(populations.shape, F32),
            vmem(2, 8, depth),
            vmem(10, width, depth),
            vmem(10, width, depth),
            vmem(2, width, depth),
            vmem(19, 4, length, depth),
            vmem(3, 6, length, depth),
        ],
        scratch_shapes=[
            pltpu.VMEM((19, width, length, depth), F32),
            pltpu.VMEM((3, 19, 4, length, depth), F32),
            pltpu.SemaphoreType.DMA((3,)),
            pltpu.SemaphoreType.DMA((4,)),
        ],
    )(*held(post, flag, rate, halo, halo_flag))

    side_near, side_far, ends, ghost, came_flag, share = call(
        second_faces,
        3,
        in_specs=whole(9),
        out_specs=whole(6),
        out_shape=[vmem(5, width + 8, depth)] * 2
        + [
            vmem(19, 2, length, depth),
            vmem(5, 2, length, depth),
            vmem(3, 2, length + 8, depth),
            vmem(count, 2, depth),
        ],
        scratch_shapes=[pltpu.VMEM((2, ROWS + 1, length, depth), F32)],
    )(*held(edge, edge_flag, edge_rate, halo_edge, halo_flag_edge, sums, side, got_far, got_near))
    side_far, side_near = exchange(side_far, side_near, "by")
    share = lax.all_to_all(share, ("bx", "by"), 0, 0)

    final = call(
        last_faces,
        6,
        in_specs=anywhere(1) + whole(10),
        out_specs=anywhere(1)[0],
        out_shape=pltpu.HBM(populations.shape, F32),
        scratch_shapes=[
            pltpu.VMEM((10, width + 8, depth), F32),
            pltpu.VMEM((2, 19, 2, length, depth), F32),
            pltpu.VMEM((10, width, 1, depth), F32),
            pltpu.SemaphoreType.DMA((2,)),
            pltpu.SemaphoreType.DMA((10,)),
        ],
        input_output_aliases={0: 0},
    )(
        *main_memory(final),
        *held(ends, after_edge, last_flag, ghost, came_flag, halo_flag_last, side_copy, own_flag),
        *held(side_near, side_far),
    )
    mean = call(
        mean_flow,
        2,
        in_specs=whole(1) + anywhere(1),
        out_specs=whole(1)[0],
        out_shape=jax.ShapeDtypeStruct((1, depth), F32),
    )(*held(share), *main_memory(final))
    return final, mean[0, :1]


def solution(mesh):
    placed = (P(None, "bx", "by", None), P("bx", "by", None), P("bx", "by", None), P())
    return jax.shard_map(
        body,
        mesh=mesh,
        in_specs=placed,
        out_specs=(P(None, "bx", "by", None), P()),
        check_vma=False,
    )
```

```python
import jax
import jax.numpy as jnp
from jax import lax
from jax.experimental import pallas as pl
from jax.experimental.pallas import tpu as pltpu
from jax.sharding import PartitionSpec as P

VELOCITY = [
    (0, 0, 0),
    (1, 0, 0),
    (-1, 0, 0),
    (0, 1, 0),
    (0, -1, 0),
    (0, 0, 1),
    (0, 0, -1),
    (1, 1, 0),
    (-1, -1, 0),
    (1, -1, 0),
    (-1, 1, 0),
    (1, 0, 1),
    (-1, 0, -1),
    (1, 0, -1),
    (-1, 0, 1),
    (0, 1, 1),
    (0, -1, -1),
    (0, 1, -1),
    (0, -1, 1),
]
OPPOSITE = [0, 2, 1, 4, 3, 6, 5, 8, 7, 10, 9, 12, 11, 14, 13, 16, 15, 18, 17]
UP_X = [q for q in range(19) if VELOCITY[q][0] == 1]
DOWN_X = [OPPOSITE[q] for q in UP_X]
UP_Y = [q for q in range(19) if VELOCITY[q][1] == 1]
DOWN_Y = [OPPOSITE[q] for q in UP_Y]
FLAG, NEXT, SUMS, RATE, ROWS = 5, 6, 11, 15, 16
GROUPS = 4
F32 = jnp.float32
MIB = 1024 * 1024


def collide(f, rate):
    rho, mx, my, mz = moments(f)
    return relax(f, rho, mx, my, mz, rate), mz


def moments(f):
    plus = {}
    diff = {}
    for q in range(1, 19, 2):
        plus[q] = f[q] + f[q + 1]
        diff[q] = f[q] - f[q + 1]
    rho = ((f[0] + plus[1]) + (plus[3] + plus[5])) + (
        ((plus[7] + plus[9]) + (plus[11] + plus[13])) + (plus[15] + plus[17])
    )
    mx = (diff[1] + diff[7]) + (diff[9] + diff[11]) + diff[13]
    my = (diff[3] + diff[7]) + (diff[15] - diff[9]) + diff[17]
    mz = (diff[5] + diff[11]) + (diff[15] - diff[13]) - diff[17]
    return rho, mx, my, mz


def relax(f, rho, mx, my, mz, rate):
    r36 = rate * (1.0 / 36.0)
    scale = r36 * (4.5 / rho)
    vx = scale * mx
    vy = scale * my
    vz = scale * mz
    tx = vx * mx
    ty = vy * my
    tz = vz * mz
    base = r36 * rho - ((tx + ty) + tz) * (1.0 / 3.0)
    keep = 1.0 - rate
    r12 = rate * (1.0 / 12.0)
    gx = r12 * mx
    gy = r12 * my
    gz = r12 * mz
    vx2 = vx + vx
    vy2 = vy + vy
    cross = {7: vx2 * my, 11: vx2 * mz, 15: vy2 * mz}
    bx = base + tx
    by = base + ty
    bz = base + tz
    pair_base = {7: bx + ty, 11: bx + tz, 15: by + tz}
    lean = {7: (gx, gy), 11: (gx, gz), 15: (gy, gz)}
    out = [None] * 19

    def put(q, even, odd):
        if f[q] is not None:
            out[q] = keep * f[q] + (even + odd)
        if f[q + 1] is not None:
            out[q + 1] = keep * f[q + 1] + (even - odd)

    if f[0] is not None:
        out[0] = keep * f[0] + 12.0 * base
    for q, b, g in ((1, bx, gx), (3, by, gy), (5, bz, gz)):
        put(q, b + b, g + g)
    for q in (7, 11, 15):
        one, two = lean[q]
        put(q, pair_base[q] + cross[q], one + two)
        put(q + 2, pair_base[q] - cross[q], one - two)
    return out


def turn(value, step):
    if step == 0:
        return value
    return pltpu.roll(value, step % value.shape[-1], axis=value.ndim - 1)


def cell_rate(cls, fluid, rates):
    rate = jnp.where(cls == 0, rates[0], rates[1])
    rate = jnp.where(cls == 2, rates[2], rate)
    rate = jnp.where(cls == 3, rates[3], rate)
    return jnp.where(fluid, rate, 0.0)


def pull(local, load, is_open):
    out = [local[0]]
    links = [None]
    for q in range(1, 19):
        links.append(is_open(q))
        out.append(jnp.where(links[q], load(q, *VELOCITY[q]), local[OPPOSITE[q]]))
    return out, links


def open_by_flag(load_flag, fluid):
    limit = jnp.where(fluid > 0.5, 0.5, 2.0)

    def is_open(q):
        move = VELOCITY[q]
        return load_flag(move[2], move[0], move[1]) > limit

    return is_open


def link_flux(post, links, mz, fluid):
    total = None
    for q in range(19):
        step = VELOCITY[q][2]
        if step == 0:
            continue
        term = jnp.where(links[OPPOSITE[q]], post[q], 0.0)
        if total is None:
            total = term if step > 0 else -term
        else:
            total = total + term if step > 0 else total - term
    return (total + total) - jnp.where(fluid > 0.5, mz, 0.0)


def beyond(ref, k, plane, g, cy, spare):
    length = ref.shape[2]
    if not spare:
        return pltpu.roll(ref[k, plane, tile(g), :], cy % 8, axis=0)
    flat = ref.reshape(ref.shape[0], ref.shape[1] * length, ref.shape[3])
    return flat[k, pl.ds(plane * length + (g * 8 - cy), 8), :]


def shifted(ref, k, plane, g, cy, low=None, high=None, spare=False, step=0):
    groups = GROUPS
    if cy == 1 and g == 0:
        value = beyond(ref, k, plane, g, cy, spare)
        if low is not None:
            value = jnp.where(lax.broadcasted_iota(jnp.int32, value.shape, 0) == 0, low(), value)
        return turn(value, step)
    if cy == -1 and g == groups - 1:
        value = beyond(ref, k, plane, g, cy, spare)
        if high is not None:
            value = jnp.where(lax.broadcasted_iota(jnp.int32, value.shape, 0) == 7, high(), value)
        return turn(value, step)
    return turn(ref[k, plane, pl.ds(g * 8 - cy, 8), :], step)


def side_row(halo_ref, x, q):
    if isinstance(x, int) and x < 0:
        x = 33
    k = UP_Y.index(q) if q in UP_Y else 5 + DOWN_Y.index(q)
    return halo_ref[k, pl.ds(x, 1), :]


def tile(g):
    return pl.ds(g * 8, 8)


def parity(axis):
    return lax.rem(lax.axis_index(axis), 2)


def first_faces(
    f_hbm, mask_hbm, cls_hbm, rates_hbm, near_ref, far_ref, rates_out,
    f_buf, mask_buf, cls_buf, rates_ref, sems, rates_sem,
):
    odd = parity("by")
    width = f_hbm.shape[1]
    length = f_hbm.shape[2]
    get_rates = pltpu.make_async_copy(rates_hbm, rates_ref, rates_sem)
    get_rates.start()
    copies = []
    for side in range(2):
        src = pl.ds(side * (length - 1), 1)
        group = [
            pltpu.make_async_copy(f_hbm.at[:, :, src, :], f_buf.at[side], sems.at[side, 0]),
            pltpu.make_async_copy(mask_hbm.at[:, src, :], mask_buf.at[side], sems.at[side, 1]),
            pltpu.make_async_copy(cls_hbm.at[:, src, :], cls_buf.at[side], sems.at[side, 2]),
        ]
        for copy in group:
            copy.start()
        copies.append(group)
    get_rates.wait()
    rates = [rates_ref[k] for k in range(4)]
    for k in range(4):
        rates_out[pl.ds(k, 1), :] = jnp.full((1, 128), rates[k], F32)
    leaving = []
    for side in range(2):
        for copy in copies[side]:
            copy.wait()
        f_rows = f_buf.at[side].reshape(19, width, 128)
        mask_rows = mask_buf.at[side].reshape(width, 128)
        cls_rows = cls_buf.at[side].reshape(width, 128)
        for g in range(width // 8):
            fluid = mask_rows[tile(g), :] == 1
            rate = cell_rate(cls_rows[tile(g), :], fluid, rates)
            post, _ = collide([f_rows[q, tile(g), :] for q in range(19)], rate)
            values = [post[q] for q in (UP_Y if side else DOWN_Y)]
            leaving.append(values + [jnp.where(fluid, 1.0, 0.0)])
    for g in range(width // 8):
        for k in range(6):
            low = leaving[g][k]
            high = leaving[width // 8 + g][k]
            far_ref[k, tile(g), :] = jnp.where(odd == 0, low, high)
            near_ref[k, tile(g), :] = jnp.where(odd == 0, high, low)


def first_step(
    f_ref, mask_ref, cls_ref, rates_ref,
    post_ref, flag_ref, rate_ref, edge_ref, edge_flag, edge_rate,
):
    width, length = mask_ref.shape[:2]
    groups = length // 8
    rates = [jnp.broadcast_to(rates_ref[pl.ds(k, 1), :], (8, 128)) for k in range(4)]

    def plane(x, carry):
        for g in range(groups):
            fluid = mask_ref[x, tile(g), :] == 1
            rate = cell_rate(cls_ref[x, tile(g), :], fluid, rates)
            post, _ = collide([f_ref[q, x, tile(g), :] for q in range(19)], rate)
            for q in range(19):
                post_ref[q, x + 1, tile(g), :] = post[q]
            rate_ref[x, tile(g), :] = rate
            flag = jnp.where(fluid, 1.0, 0.0)
            for step in (-1, 0, 1):
                flag_ref[step + 1, x + 1, tile(g), :] = turn(flag, step)
        return carry

    lax.fori_loop(0, width, plane, 0, unroll=2)
    for e, x in enumerate((0, 1, width - 2, width - 1)):
        for g in range(groups):
            for q in range(19):
                edge_ref[q, e, tile(g), :] = post_ref[q, x + 1, tile(g), :]
            for s in range(3):
                edge_flag[s, e, tile(g), :] = flag_ref[s, x + 1, tile(g), :]
    for s, x in enumerate((0, width - 1)):
        for g in range(groups):
            edge_rate[s, tile(g), :] = rate_ref[x, tile(g), :]


def join_sides(
    post_ref, edge_flag, rate_ref, near_ref, far_ref,
    far_out, near_out, halo_ref, flag_ref, halo_edge, flag_edge, flag_last, row_ref,
):
    odd_x = parity("bx")
    odd_y = parity("by")
    width = far_ref.shape[1]
    length = rate_ref.shape[1]
    groups = length // 8
    for g in range(width // 8):
        for k in range(6):
            far = far_ref[k, tile(g), :]
            near = near_ref[k, tile(g), :]
            low = jnp.where(odd_y == 0, far, near)
            high = jnp.where(odd_y == 0, near, far)
            if k < 5:
                for out_ref in (halo_ref, halo_edge):
                    out_ref[k, tile(g), :] = low
                    out_ref[5 + k, tile(g), :] = high
                continue
            for step in (-1, 0, 1):
                for side, value in enumerate((low, high)):
                    turned = turn(value, step)
                    for out_ref in (flag_ref, flag_edge, flag_last):
                        out_ref[(step + 1) * 2 + side, tile(g), :] = turned

    def outer_plane(s, g):
        own = 0 if s == 0 else 3
        plane_at = 0 if s == 0 else width - 1
        leaving = DOWN_X if s == 0 else UP_X
        arriving = UP_X if s == 0 else DOWN_X
        local = [post_ref[q, own, tile(g), :] for q in range(19)]
        rate = rate_ref[s, tile(g), :]
        fluid = edge_flag[1, own, tile(g), :]

        def load(q, cx, cy, cz):
            def beside():
                return side_row(halo_ref, plane_at - cx, q)

            return shifted(post_ref, q, own - cx, g, cy, beside, beside, step=cz)

        def load_flag(cz, cx, cy):
            return shifted(
                edge_flag, cz + 1, own - cx, g, cy,
                lambda: halo_row(flag_ref, (cz + 1) * 2, plane_at - cx),
                lambda: halo_row(flag_ref, (cz + 1) * 2 + 1, plane_at - cx),
            )

        is_open = open_by_flag(load_flag, fluid)
        f = [local[0]]
        for q in range(1, 19):
            if q in arriving:
                f.append(jnp.zeros_like(fluid))
            else:
                f.append(jnp.where(is_open(q), load(q, *VELOCITY[q]), local[OPPOSITE[q]]))
        return [local[q] for q in leaving] + [fluid] + [f[q] for q in leaving] + list(moments(f)) + [rate]

    for g in range(groups):
        low = outer_plane(0, g)
        high = outer_plane(1, g)
        for k in range(ROWS):
            far_out[k, tile(g), :] = jnp.where(odd_x == 0, low[k], high[k])
            near_out[k, tile(g), :] = jnp.where(odd_x == 0, high[k], low[k])
    for s, x in enumerate((0, width - 1)):
        leaving = DOWN_X if s == 0 else UP_X
        for q in leaving:
            if VELOCITY[q][1] != 0:
                at = 0 if VELOCITY[q][1] == 1 else 1
                row_ref[s, pl.ds(at, 1), :] = side_row(halo_ref, x, q)
        for side in range(2):
            row_ref[s, pl.ds(2 + side, 1), :] = halo_row(flag_ref, 2 + side, x)
    low = row_ref[0]
    high = row_ref[1]
    far_out[ROWS, pl.ds(0, 8), :] = jnp.where(odd_x == 0, low, high)
    near_out[ROWS, pl.ds(0, 8), :] = jnp.where(odd_x == 0, high, low)


def halo_row(ref, k, x):
    return ref[k, pl.ds(x, 1), :]


def second_inner(
    post_ref, flag_ref, rate_ref, halo_ref, halo_flag,
    out_hbm, sums_ref, side_ref, side_copy, own_flag, edge_ref, edge_flag,
    next_ref, out_buf, sems, last_sems,
):
    width, length = rate_ref.shape[:2]
    groups = length // 8
    chunk = out_buf.shape[2]
    slots = out_buf.shape[0]

    def collide_tile(x, g, carry):
        flux, count = carry
        local = [post_ref[q, x + 1, tile(g), :] for q in range(19)]
        fluid = flag_ref[1, x + 1, tile(g), :]

        def load(q, cx, cy, cz):
            def side():
                return side_row(halo_ref, x - cx, q)

            return shifted(post_ref, q, x + 1 - cx, g, cy, side, side, spare=True, step=cz)

        def load_flag(cz, cx, cy):
            return shifted(
                flag_ref, cz + 1, x + 1 - cx, g, cy,
                lambda: halo_row(halo_flag, (cz + 1) * 2, x - cx),
                lambda: halo_row(halo_flag, (cz + 1) * 2 + 1, x - cx),
                spare=True,
            )

        f, links = pull(local, load, open_by_flag(load_flag, fluid))
        post, mz = collide(f, rate_ref[x, tile(g), :])
        for q in range(19):
            next_ref[q, x, tile(g), :] = post[q]
        flux = flux + link_flux(post, links, mz, fluid)
        count = count + fluid
        return flux, count

    def stream_tile(x, g, slot, j):
        local = [next_ref[q, x, tile(g), :] for q in range(19)]

        def load(q, cx, cy, cz):
            return shifted(next_ref, q, x - cx, g, cy, spare=True, step=cz)

        def load_flag(cz, cx, cy):
            return shifted(flag_ref, cz + 1, x + 1 - cx, g, cy, spare=True)

        f, _ = pull(local, load, open_by_flag(load_flag, flag_ref[1, x + 1, tile(g), :]))
        for q in range(19):
            out_buf[slot, q, j, tile(g), :] = f[q]

    def copy_out(c):
        slot = lax.rem(c, slots)
        return pltpu.make_async_copy(
            out_buf.at[slot], out_hbm.at[:, pl.ds(2 + c * chunk, chunk)], sems.at[slot]
        )

    def first(x, carry):
        for g in range(groups):
            carry = collide_tile(x, g, carry)
        return carry

    zero = jnp.zeros((8, 128), F32)
    carry = lax.fori_loop(1, 4, first, (zero, zero), unroll=3)
    parts = (width - 4) // chunk

    def part(c, carry):
        slot = lax.rem(c, slots)

        @pl.when(c >= slots)
        def _():
            copy_out(c - slots).wait()

        def step(j, carry):
            x = 2 + c * chunk + j
            for g in range(groups):
                stream_tile(x, g, slot, j)
            for g in range(groups):
                carry = collide_tile(x + 2, g, carry)
            return carry

        carry = lax.fori_loop(0, chunk, step, carry, unroll=chunk)
        copy_out(c).start()
        return carry

    carry = lax.fori_loop(0, parts - 1, part, carry)
    last_slot = (parts - 1) % slots
    last_x = 2 + (parts - 1) * chunk

    def copy_last(j, planes):
        return pltpu.make_async_copy(
            out_buf.at[last_slot, :, pl.ds(j, planes)],
            out_hbm.at[:, pl.ds(last_x + j, planes)],
            last_sems.at[j],
        )

    @pl.when(parts > slots)
    def _():
        copy_out(parts - 1 - slots).wait()

    for j in range(chunk):
        x = last_x + j
        for g in range(groups):
            stream_tile(x, g, last_slot, j)
        copy_last(j, 1).start()
        for g in range(groups if j < chunk - 1 else 0):
            carry = collide_tile(x + 2, g, carry)
    flux, count = carry
    sums_ref[0] = flux
    sums_ref[1] = count
    pitch = next_ref.shape[2]
    flat = next_ref.reshape(19, width * pitch, 128)
    flags = flag_ref.reshape(3, (width + 2) * pitch, 128)
    for g in range(width // 8):
        low_at = pl.ds(g * 8 * pitch, 8, stride=pitch)
        high_at = pl.ds(g * 8 * pitch + length - 1, 8, stride=pitch)
        for k in range(5):
            low = flat[DOWN_Y[k], low_at, :]
            high = flat[UP_Y[k], high_at, :]
            for to_ref in (side_ref, side_copy):
                to_ref[k, tile(g), :] = low
                to_ref[5 + k, tile(g), :] = high
        own_flag[0, tile(g), :] = flags[1, pl.ds((g * 8 + 1) * pitch, 8, stride=pitch), :]
        own_flag[1, tile(g), :] = flags[1, pl.ds((g * 8 + 1) * pitch + length - 1, 8, stride=pitch), :]
    for e, x in enumerate((1, 2, width - 3, width - 2)):
        for g in range(groups):
            for q in range(19):
                edge_ref[q, e, tile(g), :] = next_ref[q, x, tile(g), :]
    for e, x in enumerate((0, 1, 2, width - 3, width - 2, width - 1)):
        for g in range(groups):
            for s in range(3):
                edge_flag[s, e, tile(g), :] = flag_ref[s, x + 1, tile(g), :]
    for c in range(parts - slots, parts - 1):
        copy_out(c).wait()
    for j in range(chunk):
        copy_last(j, 1).wait()


def second_faces(
    post_ref, flag_ref, rate_ref, halo_ref, halo_flag, sums_ref, side_ref, far_ref, near_ref,
    side_near, side_far, ends_ref, ghost_ref, came_flag, share_ref, came_ref,
):
    odd_x = parity("bx")
    odd_y = parity("by")
    length = rate_ref.shape[1]
    width = side_ref.shape[1]
    groups = length // 8
    flux = sums_ref[0]
    count = sums_ref[1]
    for k in range(ROWS + 1):
        for g in range(groups if k < ROWS else 1):
            far = far_ref[k, tile(g), :]
            near = near_ref[k, tile(g), :]
            came_ref[0, k, tile(g), :] = jnp.where(odd_x == 0, far, near)
            came_ref[1, k, tile(g), :] = jnp.where(odd_x == 0, near, far)
    for s, side in enumerate((1, -1)):
        plane_at = 0 if s == 0 else width - 1
        group = UP_X if side == 1 else DOWN_X
        own = 0 if s == 0 else 3

        for step in (-1, 0, 1):
            for g in range(groups):
                came_flag[step + 1, s, pl.ds(1 + g * 8, 8), :] = turn(came_ref[s, FLAG, tile(g), :], step)
            for end in range(2):
                row = turn(came_ref[s, ROWS, pl.ds(2 + end, 1), :], step)
                came_flag[step + 1, s, pl.ds(end * (length + 1), 1), :] = row
        for g in range(groups):
            local = [post_ref[q, own, tile(g), :] for q in range(19)]
            fluid = flag_ref[1, own, tile(g), :]

            def load(q, cx, cy, cz):
                def beside():
                    return side_row(halo_ref, plane_at - cx, q)

                if cx == side:
                    return shifted(
                        came_ref, s, group.index(q), g, cy,
                        lambda: came_ref[s, ROWS, pl.ds(0, 1), :],
                        lambda: came_ref[s, ROWS, pl.ds(1, 1), :],
                        step=cz,
                    )
                return shifted(post_ref, q, own - cx, g, cy, beside, beside, step=cz)

            def load_flag(cz, cx, cy):
                if cx == side:
                    return came_flag[cz + 1, s, pl.ds(1 + g * 8 - cy, 8), :]
                return shifted(
                    flag_ref, cz + 1, own - cx, g, cy,
                    lambda: halo_row(halo_flag, (cz + 1) * 2, plane_at - cx),
                    lambda: halo_row(halo_flag, (cz + 1) * 2 + 1, plane_at - cx),
                )

            f, links = pull(local, load, open_by_flag(load_flag, fluid))
            post, mz = collide(f, rate_ref[s, tile(g), :])
            for q in range(19):
                ends_ref[q, s, tile(g), :] = post[q]
            flux = flux + link_flux(post, links, mz, fluid)
            count = count + fluid

            beyond_fluid = came_ref[s, FLAG, tile(g), :]
            rho, mx, my, mz = [came_ref[s, SUMS + i, tile(g), :] for i in range(4)]

            def own_flag(cz, cx, cy):
                return shifted(
                    flag_ref, cz + 1, own, g, cy,
                    lambda: halo_row(halo_flag, (cz + 1) * 2, plane_at),
                    lambda: halo_row(halo_flag, (cz + 1) * 2 + 1, plane_at),
                )

            is_open = open_by_flag(own_flag, beyond_fluid)
            for k, toward in enumerate(group):
                q = OPPOSITE[toward]
                _, cy, cz = VELOCITY[q]

                def beside():
                    return side_row(halo_ref, plane_at, q)

                source = shifted(post_ref, q, own, g, cy, beside, beside, step=cz)
                value = jnp.where(is_open(q), source, came_ref[s, k, tile(g), :])
                rho = rho + value
                mx = mx - value if side == 1 else mx + value
                if cy != 0:
                    my = my + value if cy == 1 else my - value
                if cz != 0:
                    mz = mz + value if cz == 1 else mz - value
            f = [None] * 19
            for k, q in enumerate(group):
                f[q] = came_ref[s, NEXT + k, tile(g), :]
            post = relax(f, rho, mx, my, mz, came_ref[s, RATE, tile(g), :])
            for k, q in enumerate(group):
                ghost_ref[k, s, tile(g), :] = post[q]

    for k in range(5):
        for g in range(width // 8):
            low = side_ref[k, tile(g), :]
            high = side_ref[5 + k, tile(g), :]
            side_far[k, tile(g), :] = jnp.where(odd_y == 0, low, high)
            side_near[k, tile(g), :] = jnp.where(odd_y == 0, high, low)
        for s, x in enumerate((0, width - 1)):
            low = ends_ref[DOWN_Y[k], s, pl.ds(0, 1), :]
            high = ends_ref[UP_Y[k], s, pl.ds(length - 1, 1), :]
            side_far[k, pl.ds(x, 1), :] = jnp.where(odd_y == 0, low, high)
            side_near[k, pl.ds(x, 1), :] = jnp.where(odd_y == 0, high, low)
        for s, group, x in ((0, UP_X, width + 1), (1, DOWN_X, width)):
            if DOWN_Y[k] in group:
                low = ghost_ref[group.index(DOWN_Y[k]), s, pl.ds(0, 1), :]
                side_far[k, pl.ds(x, 1), :] = low
                side_near[k, pl.ds(x, 1), :] = low
    for k in range(5):
        for s, group, x in ((0, UP_X, width + 1), (1, DOWN_X, width)):
            if UP_Y[k] in group:
                high = ghost_ref[group.index(UP_Y[k]), s, pl.ds(length - 1, 1), :]
                out_low = side_far[k, pl.ds(x, 1), :]
                side_far[k, pl.ds(x, 1), :] = jnp.where(odd_y == 0, out_low, high)
                side_near[k, pl.ds(x, 1), :] = jnp.where(odd_y == 0, high, out_low)
    lane = lax.broadcasted_iota(jnp.int32, (1, 128), 1)
    total = jnp.sum(jnp.sum(flux, axis=0, keepdims=True), axis=1, keepdims=True)
    cells = jnp.sum(jnp.sum(count, axis=0, keepdims=True), axis=1, keepdims=True)
    row = jnp.where(lane < 64, total, cells)
    share_ref[...] = jnp.broadcast_to(row[None], share_ref.shape)


def mean_flow(share_ref, order_ref, mean_ref):
    del order_ref
    total = jnp.sum(share_ref[:, 0, :], axis=0, keepdims=True)
    lane = lax.broadcasted_iota(jnp.int32, (1, 128), 1)
    flux = jnp.sum(jnp.where(lane == 0, total, 0.0), axis=1, keepdims=True)
    cells = jnp.sum(jnp.where(lane == 127, total, 0.0), axis=1, keepdims=True)
    mean_ref[...] = jnp.broadcast_to(flux / cells, mean_ref.shape)


def last_faces(
    out_in, ends_ref, edge_ref, edge_flag, ghost_ref, came_flag, halo_flag, side_ref, own_flag,
    side_near, side_far,
    out_hbm, halo_ref, out_buf, row_buf, sems, row_sems,
):
    del out_in
    odd_y = parity("by")
    width, length = out_hbm.shape[1:3]
    groups = length // 8
    copies = []
    for k in range(5):
        for g in range(width // 8 + 1):
            far = side_far[k, tile(g), :]
            near = side_near[k, tile(g), :]
            halo_ref[k, tile(g), :] = jnp.where(odd_y == 0, far, near)
            halo_ref[5 + k, tile(g), :] = jnp.where(odd_y == 0, near, far)

    for side, group in enumerate((UP_Y, DOWN_Y)):
        for k, q in enumerate(group):
            cx, _, cz = VELOCITY[q]
            for x in (1, 9, 17, width - 9):
                fluid = own_flag[side, pl.ds(x, 8), :]
                limit = jnp.where(fluid > 0.5, 0.5, 2.0)
                is_open = halo_flag[(cz + 1) * 2 + side, pl.ds(x - cx, 8), :] > limit
                source = turn(halo_ref[side * 5 + k, pl.ds(x - cx, 8), :], cz)
                value = jnp.where(is_open, source, side_ref[side * 5 + k, pl.ds(x, 8), :])
                row_buf[side * 5 + k, pl.ds(x, 8), 0, :] = value
            planes = pl.ds(2, width - 4)
            copy = pltpu.make_async_copy(
                row_buf.at[side * 5 + k, planes],
                out_hbm.at[q, planes, pl.ds(side * (length - 1), 1), :],
                row_sems.at[side * 5 + k],
            )
            copy.start()
            copies.append(copy)

    for s, side in enumerate((1, -1)):
        group = UP_X if side == 1 else DOWN_X
        for outer in (0, 1):
            plane_at = outer if s == 0 else width - 1 - outer
            for g in range(groups):

                def at(plane):
                    if plane == 0:
                        return ends_ref, s
                    return edge_ref, plane - 1 if s == 0 else 4 - plane

                own_ref, own = at(outer)
                local = [own_ref[q, own, tile(g), :] for q in range(19)]

                def load(q, cx, cy, cz):
                    def beside():
                        return side_row(halo_ref, plane_at - cx, q)

                    plane = outer - cx * side
                    if plane < 0:
                        return shifted(ghost_ref, group.index(q), s, g, cy, beside, beside, step=cz)
                    ref, index = at(plane)
                    return shifted(ref, q, index, g, cy, beside, beside, step=cz)

                def load_flag(cz, cx, cy):
                    plane = outer - cx * side
                    if plane < 0:
                        return came_flag[cz + 1, s, pl.ds(1 + g * 8 - cy, 8), :]
                    return shifted(
                        edge_flag, cz + 1, plane if s == 0 else 5 - plane, g, cy,
                        lambda: halo_row(halo_flag, (cz + 1) * 2, plane_at - cx),
                        lambda: halo_row(halo_flag, (cz + 1) * 2 + 1, plane_at - cx),
                    )

                fluid = edge_flag[1, outer if s == 0 else 5 - outer, tile(g), :]
                f, _ = pull(local, load, open_by_flag(load_flag, fluid))
                for q in range(19):
                    out_buf[s, q, outer if s == 0 else 1 - outer, tile(g), :] = f[q]
        planes = pl.ds(0 if s == 0 else width - 2, 2)
        copy = pltpu.make_async_copy(out_buf.at[s], out_hbm.at[:, planes], sems.at[s])
        copy.start()
        copies.append(copy)
    for copy in copies:
        copy.wait()


def whole(count=1):
    return [pl.BlockSpec(memory_space=pltpu.VMEM)] * count


def anywhere(count=1):
    return [pl.BlockSpec(memory_space=pl.ANY)] * count


def vmem(*shape):
    return pltpu.VMEM(shape, F32)


def held(*arrays):
    return [pltpu.with_memory_space_constraint(a, pltpu.VMEM) for a in arrays]


def main_memory(*arrays):
    return [pltpu.with_memory_space_constraint(a, pltpu.HBM) for a in arrays]


def call(kernel, scratch_mib, kib=0, **kwargs):
    return pl.pallas_call(
        kernel,
        cost_estimate=pl.CostEstimate(flops=0, bytes_accessed=kib * 1024, transcendentals=0),
        compiler_params=pltpu.CompilerParams(vmem_limit_bytes=scratch_mib * MIB),
        name=kernel.__name__,
        **kwargs,
    )


def pairs_of(count):
    far = [(i, (i + 1) % count if i % 2 else (i - 1) % count) for i in range(count)]
    near = [(i, i ^ 1) for i in range(count)]
    return far, near


def exchange(far, near, axis):
    far_pairs, near_pairs = pairs_of(lax.axis_size(axis))
    return lax.ppermute(far, axis, far_pairs), lax.ppermute(near, axis, near_pairs)


def body(populations, fluid_mask, rate_class, class_rates):
    width, length, depth = fluid_mask.shape
    count = lax.axis_size("bx") * lax.axis_size("by")
    given = main_memory(populations, fluid_mask, rate_class, class_rates)

    near, far, rates = call(
        first_faces,
        7,
        16384,
        in_specs=anywhere(4),
        out_specs=whole(3),
        out_shape=[vmem(6, width, depth)] * 2 + [vmem(8, depth)],
        scratch_shapes=[
            pltpu.VMEM((2, 19, width, 1, depth), F32),
            pltpu.VMEM((2, width, 1, depth), jnp.int32),
            pltpu.VMEM((2, width, 1, depth), jnp.int32),
            pltpu.SMEM((4,), F32),
            pltpu.SemaphoreType.DMA((2, 3)),
            pltpu.SemaphoreType.DMA,
        ],
    )(*given)
    got_far, got_near = exchange(far, near, "by")

    post, flag, rate, edge, edge_flag, edge_rate = call(
        first_step,
        2,
        in_specs=whole(4),
        out_specs=whole(6),
        out_shape=[
            vmem(19, width + 2, length + 8, depth),
            vmem(3, width + 2, length + 8, depth),
            vmem(width, length, depth),
            vmem(19, 4, length, depth),
            vmem(3, 4, length, depth),
            vmem(2, length, depth),
        ],
    )(*held(populations, fluid_mask, rate_class, rates))

    far, near, halo, halo_flag, halo_edge, halo_flag_edge, halo_flag_last = call(
        join_sides,
        2,
        in_specs=whole(5),
        out_specs=whole(7),
        out_shape=[vmem(ROWS + 1, length, depth)] * 2
        + [vmem(10, width, depth), vmem(6, width, depth)] * 2
        + [vmem(6, width, depth)],
        scratch_shapes=[pltpu.VMEM((2, 8, depth), F32)],
    )(*held(edge, edge_flag, edge_rate, got_near, got_far))
    got_far, got_near = exchange(far, near, "bx")

    final, sums, side, side_copy, own_flag, after_edge, last_flag = call(
        second_inner,
        20,
        in_specs=whole(5),
        out_specs=anywhere(1) + whole(6),
        out_shape=[
            pltpu.HBM(populations.shape, F32),
            vmem(2, 8, depth),
            vmem(10, width, depth),
            vmem(10, width, depth),
            vmem(2, width, depth),
            vmem(19, 4, length, depth),
            vmem(3, 6, length, depth),
        ],
        scratch_shapes=[
            pltpu.VMEM((19, width, length + 8, depth), F32),
            pltpu.VMEM((3, 19, 4, length, depth), F32),
            pltpu.SemaphoreType.DMA((3,)),
            pltpu.SemaphoreType.DMA((4,)),
        ],
    )(*held(post, flag, rate, halo, halo_flag))

    side_near, side_far, ends, ghost, came_flag, share = call(
        second_faces,
        3,
        in_specs=whole(9),
        out_specs=whole(6),
        out_shape=[vmem(5, width + 8, depth)] * 2
        + [
            vmem(19, 2, length, depth),
            vmem(5, 2, length, depth),
            vmem(3, 2, length + 8, depth),
            vmem(count, 2, depth),
        ],
        scratch_shapes=[pltpu.VMEM((2, ROWS + 1, length, depth), F32)],
    )(*held(edge, edge_flag, edge_rate, halo_edge, halo_flag_edge, sums, side, got_far, got_near))
    side_far, side_near = exchange(side_far, side_near, "by")
    share = lax.all_to_all(share, ("bx", "by"), 0, 0)

    final = call(
        last_faces,
        6,
        in_specs=anywhere(1) + whole(10),
        out_specs=anywhere(1)[0],
        out_shape=pltpu.HBM(populations.shape, F32),
        scratch_shapes=[
            pltpu.VMEM((10, width + 8, depth), F32),
            pltpu.VMEM((2, 19, 2, length, depth), F32),
            pltpu.VMEM((10, width, 1, depth), F32),
            pltpu.SemaphoreType.DMA((2,)),
            pltpu.SemaphoreType.DMA((10,)),
        ],
        input_output_aliases={0: 0},
    )(
        *main_memory(final),
        *held(ends, after_edge, last_flag, ghost, came_flag, halo_flag_last, side_copy, own_flag),
        *held(side_near, side_far),
    )
    mean = call(
        mean_flow,
        2,
        in_specs=whole(1) + anywhere(1),
        out_specs=whole(1)[0],
        out_shape=jax.ShapeDtypeStruct((1, depth), F32),
    )(*held(share), *main_memory(final))
    return final, mean[0, :1]


def solution(mesh):
    placed = (P(None, "bx", "by", None), P("bx", "by", None), P("bx", "by", None), P())
    return jax.shard_map(
        body,
        mesh=mesh,
        in_specs=placed,
        out_specs=(P(None, "bx", "by", None), P()),
        check_vma=False,
    )
```
